256 devices in a mesh: row: 16 (over y, z_hi, core), col: 16 (over x, z_lo).
Axes of the slice: x: 4, y: 4, z: 8 (z_hi: 2, z_lo: 4; z = z_hi * 4 + z_lo), core: 2. Of those that a mesh axis runs over, the one named last changes fastest.
Arguments:
- vectors: float32 [16, 393216], P(None, ('row', 'col')), may hold values from -6 to 6
- tiles: float32 [16, 16, 48, 256, 256], P('row', 'col'), may hold values from -0.375 to 0.375
- tile_rows: int32 [16, 16, 48], P('row', 'col'), may hold values from 0 to 95, as said below
- tile_cols: int32 [16, 16, 48], P('row', 'col'), may hold values from 0 to 95, as said below
- counts: int32 [16, 16], P('row', 'col'), may hold values from 6 to 48, as said below
Outputs:
- residual: float32 [16, 393216], P(None, ('row', 'col'))
- image: float32 [16, 393216], P(None, ('row', 'col'))
- gram: float32 [16, 16], replicated
The draws below stay inside these ranges and needn't reach their ends.
Inputs may be any that keep to these rules, and one draw needn't show every extreme that they name: Within one cell the slots name distinct tile positions. The live slots of one cell name at most 3 distinct block rows within any one segment (tile_rows // 6 equal), and every cell has a segment with exactly 3. The live slots of one cell name at most 3 distinct block columns within any one segment (tile_cols // 6 equal), and every cell has a segment with exactly 3. `counts`: some cell holds all 48 slots live in every draw; slots at or above a cell's count hold unused tiles.
All inputs are finite; a program needn't handle non-finite values.
Results may differ from the reference program's by a relative error of at most 0.0001.
Values sent between devices are 32-bit elements; how exact they have to be, the bound alone decides.
No kernel may reach another device: no remote copies, remote signals or barrier semaphores. Data moves between devices by JAX's collectives and lax.ppermute only.
A program may use at most 64 MiB of HBM per device.

```python
import jax
import jax.numpy as jnp
from jax import lax

NV = 16
TILE = 256
SEGB = 6
MAXT = 48
CAP = 3
ORDER = 393216
N_ROW = 16
N_COL = 16


def draw_positions(key):
    row_space = N_COL * CAP
    col_space = N_ROW * CAP
    total = row_space * col_space
    keys = jax.random.split(key, N_ROW * N_COL)
    cell_ids = jnp.arange(N_ROW * N_COL, dtype=jnp.int32)
    forced_index = jnp.arange(CAP, dtype=jnp.int32)
    forced = ((N_COL - 1) * CAP + forced_index) * col_space + (N_ROW - 1) * CAP + forced_index

    def one_cell(single, cell):
        first, second, third = jax.random.split(single, 3)
        scores = jax.random.permutation(first, total).astype(jnp.int32)
        scores = scores.at[forced].set(-1 - forced_index)
        picked = jnp.argsort(scores, stable=True)[:MAXT].astype(jnp.int32)
        row_comp = picked // col_space
        col_comp = picked % col_space
        row_shift = jax.random.randint(second, (), 0, SEGB)
        col_shift = jax.random.randint(third, (), 0, SEGB)
        row_shift = jnp.where(cell == 0, SEGB - CAP, row_shift)
        col_shift = jnp.where(cell == 0, SEGB - CAP, col_shift)
        rows = row_comp // CAP * SEGB + (row_comp % CAP + row_shift) % SEGB
        cols = col_comp // CAP * SEGB + (col_comp % CAP + col_shift) % SEGB
        return (rows.astype(jnp.int32), cols.astype(jnp.int32))
    rows, cols = jax.vmap(one_cell)(keys, cell_ids)
    return (rows.reshape(N_ROW, N_COL, MAXT), cols.reshape(N_ROW, N_COL, MAXT))


def draw_tile_rows(key, part):
    rows, cols = draw_positions(key)
    return rows.astype(jnp.int32)


def draw_tile_cols(key, part):
    rows, cols = draw_positions(key)
    return cols.astype(jnp.int32)


def draw_counts(key, part):
    key = jax.random.fold_in(key, 7)
    first, second, third = jax.random.split(key, 3)
    base = jax.random.randint(first, (N_ROW, N_COL), MAXT // 8, MAXT // 3 + 1)
    heavy = jax.random.randint(second, (N_ROW, N_COL), 0, 16) == 0
    base = jnp.where(heavy, MAXT, base)
    where_full = jax.random.randint(third, (), 0, N_ROW * N_COL)
    flat = base.reshape(-1).at[where_full].set(MAXT)
    return flat.reshape(N_ROW, N_COL).astype(jnp.int32)


def shard_levels(key, dims, shards, smallest, largest):
    def one(dim, shards_of):
        heights = jax.random.uniform(jax.random.fold_in(jax.random.fold_in(key, 6), dim), (shards_of,), jnp.float32, smallest / len(shards), largest / len(shards))
        return jnp.repeat(jnp.exp(heights), dims[dim] // shards_of).reshape((-1,) + (1,) * (len(dims) - dim - 1))

    factor_of = one(*shards[0])
    for cut in shards[1:]:
        factor_of = factor_of * one(*cut)
    return factor_of


def normal_values(rng, extent, scale, limit, shards=(), kind=jnp.bfloat16):
    values = scale * jax.random.normal(rng, extent, jnp.float32)
    if shards:
        values = values * shard_levels(rng, extent, shards, -0.22, 0.18)
    return jnp.clip(values, -limit, limit).astype(kind)


def setup_inputs(seed: int = 0) -> dict:
    seeds = jax.random.split(jax.random.key(seed), 6)
    return {
        "vectors": normal_values(seeds[0], (NV, ORDER), 1.0, 6.0, ((1, 256),), jnp.float32),
        "tiles": normal_values(seeds[1], (N_ROW, N_COL, MAXT, TILE, TILE), TILE ** -0.5, 0.375, ((0, 16), (1, 16)), jnp.float32),
        "tile_rows": draw_tile_rows(jax.random.fold_in(seeds[5], 71), 0),
        "tile_cols": draw_tile_cols(jax.random.fold_in(seeds[5], 71), 0),
        "counts": draw_counts(jax.random.fold_in(seeds[5], 71), 0),
    }


def block_indices(tile_rows, tile_cols):
    row_ids = jnp.arange(N_ROW, dtype=jnp.int32)[:, None, None]
    col_ids = jnp.arange(N_COL, dtype=jnp.int32)[None, :, None]
    global_rows = row_ids * (N_COL * SEGB) + tile_rows
    global_cols = (tile_cols // SEGB * N_COL + col_ids) * SEGB + tile_cols % SEGB
    return (global_rows.astype(jnp.int32), global_cols.astype(jnp.int32))

def apply_hamiltonian(block, tiles, global_rows, global_cols, live):
    blocks = block.reshape(NV, ORDER // TILE, TILE)
    flat_tiles = tiles.reshape(N_ROW * N_COL, MAXT, TILE, TILE)
    flat_rows = global_rows.reshape(N_ROW * N_COL, MAXT)
    flat_cols = global_cols.reshape(N_ROW * N_COL, MAXT)
    flat_live = live.reshape(N_ROW * N_COL, MAXT)

    def step(total, items):
        cell_tiles, rows, cols, alive = items
        masked = cell_tiles * alive[:, None, None]
        from_cols = blocks[:, cols, :]
        from_rows = blocks[:, rows, :]
        to_rows = jnp.einsum('kij,vkj->vki', masked, from_cols, precision=lax.Precision.HIGHEST)
        to_cols = jnp.einsum('kij,vki->vkj', masked, from_rows, precision=lax.Precision.HIGHEST)
        total = total.at[:, rows, :].add(to_rows)
        total = total.at[:, cols, :].add(to_cols)
        return (total, None)
    start = jnp.zeros((NV, ORDER // TILE, TILE), jnp.float32)
    total, unused = lax.scan(step, start, (flat_tiles, flat_rows, flat_cols, flat_live))
    return total.reshape(NV, ORDER)

def reference(vectors, tiles, tile_rows, tile_cols, counts):
    global_rows, global_cols = block_indices(tile_rows, tile_cols)
    slots = jnp.arange(MAXT, dtype=jnp.int32)[None, None, :]
    live = (slots < counts[:, :, None]).astype(jnp.float32)
    product = apply_hamiltonian(vectors, tiles, global_rows, global_cols, live)
    correlation = jnp.einsum('vn,wn->vw', vectors, vectors, precision=lax.Precision.HIGHEST)
    projection = jnp.einsum('vn,wn->vw', vectors, product, precision=lax.Precision.HIGHEST)
    factor = jnp.linalg.cholesky(correlation)
    coeffs = jax.scipy.linalg.cho_solve((factor, True), projection)
    residual = product - jnp.einsum('wv,wn->vn', coeffs, vectors, precision=lax.Precision.HIGHEST)
    image = apply_hamiltonian(residual, tiles, global_rows, global_cols, live)
    gram = jnp.einsum('vn,wn->vw', residual, image, precision=lax.Precision.HIGHEST) / ORDER
    return (residual, image, gram)
```

```python
import jax
import jax.numpy as jnp
from jax import lax
from jax.experimental import pallas as pl
from jax.experimental.pallas import tpu as pltpu
from jax.sharding import PartitionSpec as P


NV = 16
TILE = 256
SEGB = 6
CAP = 3
SEG = SEGB * NV
RID = 8
F32 = jnp.float32
BF16 = jnp.bfloat16
HIGH = lax.Precision.HIGHEST
VMEM_LIMIT = 48 * 1024 * 1024


def vspec():
    return pl.BlockSpec(memory_space=pltpu.VMEM)


def sspec():
    return pl.BlockSpec(memory_space=pltpu.SMEM)


def params():
    return pltpu.CompilerParams(vmem_limit_bytes=VMEM_LIMIT)


def row_shift(step):
    return [(i, (i // 4 + step) % 4 * 4 + i % 4) for i in range(16)]


OTHER_HALF = [(i, i ^ 2) for i in range(16)]
OTHER_CORE = [(i, i ^ 1) for i in range(16)]


def prep_kernel(place, rows, cols, counts, vectors, seg, table, slots, mark, used):
    n_segs = table.shape[0]

    def clear(b, _):
        mark[b] = -1
        return 0

    lax.fori_loop(0, n_segs * SEGB, clear, 0)

    def clear_table(s, _):
        used[s] = 0
        for q in range(CAP):
            table[s, q] = 0
        return 0

    lax.fori_loop(0, n_segs, clear_table, 0)
    my_y, my_half, my_core = place[0] // 4, place[0] // 2 % 2, place[0] % 2

    def slot(k, _):
        b = rows[0, 0, k]
        s = b // SEGB
        old = mark[b]
        rank = jnp.where(old < 0, used[s], old)
        mark[b] = rank
        used[s] = jnp.where(old < 0, rank + 1, used[s])
        table[s, rank] = b - s * SEGB
        slots[0, k] = s * CAP + rank
        g = cols[0, 0, k]
        t = g // SEGB
        step = (t // 4 + 4 - my_y) % 4
        half = (t // 2 % 2 + my_half) % 2
        core = (t % 2 + my_core) % 2
        slots[1, k] = ((core * 4 + step) * 2 + half) * SEGB + g - t * SEGB
        return 0

    lax.fori_loop(0, counts[0, 0], slot, 0)
    for b in range(SEGB):
        seg[b * NV : (b + 1) * NV, :] = vectors[:, b * TILE : (b + 1) * TILE]


def prep(vectors, rows, cols, counts, place):
    n_segs = lax.axis_size("col")
    slots = rows.shape[-1]
    return pl.pallas_call(
        prep_kernel,
        out_shape=(
            jax.ShapeDtypeStruct((SEG, TILE), F32),
            jax.ShapeDtypeStruct((n_segs, 128), jnp.int32),
            jax.ShapeDtypeStruct((2, slots), jnp.int32),
        ),
        in_specs=[sspec()] * 4 + [vspec()],
        out_specs=(vspec(), sspec(), sspec()),
        scratch_shapes=[pltpu.SMEM((n_segs * SEGB,), jnp.int32), pltpu.SMEM((n_segs,), jnp.int32)],
        compiler_params=params(),
        name="prep",
    )(place, rows, cols, counts, vectors)


def pack_into(wanted, seg, message):
    for d in range(message.shape[0]):
        for q in range(CAP):
            b = wanted[d, q]
            message[d, q * NV : (q + 1) * NV, :] = seg[pl.ds(pl.multiple_of(b * NV, NV), NV), :]


def pack_kernel(wanted, seg, message):
    pack_into(wanted, seg, message)


def pack(wanted, seg):
    return pl.pallas_call(
        pack_kernel,
        out_shape=jax.ShapeDtypeStruct((wanted.shape[0], CAP * NV, TILE), F32),
        in_specs=[sspec(), vspec()],
        out_specs=vspec(),
        compiler_params=params(),
        name="pack",
    )(wanted, seg)


def split(x):
    high = x.astype(BF16)
    return high, (x - high.astype(F32)).astype(BF16)


def product_kernel(rider, *refs):
    counts, slots, tiles, from_x = refs[:4]
    from_y = refs[4:12]
    to_x = refs[12]
    to_y = refs[13:21]
    held, sems, row_vecs, col_vecs, row_sum, col_sum = refs[21:]
    count = counts[0, 0]

    def copy(k):
        return pltpu.make_async_copy(tiles.at[k], held.at[k], sems.at[k])

    def start(k, _):
        copy(k).start()
        return 0

    lax.fori_loop(0, count, start, 0)
    n_segs = from_x.shape[0]
    for s in range(n_segs):
        for q in range(CAP):
            high, low = split(from_x[s, q * NV : (q + 1) * NV, :])
            row_vecs[s * CAP + q, 0:NV, :] = high
            row_vecs[s * CAP + q, NV : 2 * NV, :] = low
            row_sum[s * CAP + q] = jnp.zeros((NV, TILE), F32)
    for p in range(8):
        for b in range(2 * SEGB):
            high, low = split(from_y[p][b * NV : (b + 1) * NV, :])
            col_vecs[p * 2 * SEGB + b, 0:NV, :] = high
            col_vecs[p * 2 * SEGB + b, NV : 2 * NV, :] = low
            col_sum[p * 2 * SEGB + b] = jnp.zeros((NV, TILE), F32)

    def slot(k, _):
        copy(k).wait()
        i = slots[0, k]
        j = slots[1, k]
        high, low = split(held[k])
        v_row = row_vecs[i]
        v_col = col_vecs[j]
        across = (((1,), (1,)), ((), ()))
        a = lax.dot_general(v_col, high, across, preferred_element_type=F32)
        b = lax.dot_general(v_col[:NV], low, across, preferred_element_type=F32)
        row_sum[i] += a[:NV] + a[NV:] + b
        c = jnp.dot(v_row, high, preferred_element_type=F32)
        d = jnp.dot(v_row[:NV], low, preferred_element_type=F32)
        col_sum[j] += c[:NV] + c[NV:] + d
        return 0

    lax.fori_loop(0, count, slot, 0)
    if rider:
        carried = from_y[0][2 * SEG : 2 * SEG + RID, :]
        for p in range(1, 8):
            carried = carried + from_y[p][2 * SEG : 2 * SEG + RID, :]
    for s in range(n_segs):
        for q in range(CAP):
            to_x[s, q * NV : (q + 1) * NV, :] = row_sum[s * CAP + q]
        if rider:
            to_x[s, CAP * NV : CAP * NV + RID, :] = carried
    for p in range(8):
        for b in range(2 * SEGB):
            to_y[p][b * NV : (b + 1) * NV, :] = col_sum[p * 2 * SEGB + b]


def cell_product(counts, slots, tiles, from_x, from_y, rider):
    n_segs = from_x.shape[0]
    maxt = tiles.shape[0]
    rows = CAP * NV + (RID if rider else 0)

    def kernel(*refs):
        product_kernel(rider, *refs)

    return pl.pallas_call(
        kernel,
        out_shape=(jax.ShapeDtypeStruct((n_segs, rows, TILE), F32),)
        + (jax.ShapeDtypeStruct((2 * SEG, TILE), F32),) * 8,
        in_specs=[sspec(), sspec(), pl.BlockSpec(memory_space=pl.ANY)] + [vspec()] * 9,
        out_specs=(vspec(),) * 9,
        scratch_shapes=[
            pltpu.VMEM((maxt, TILE, TILE), F32),
            pltpu.SemaphoreType.DMA((maxt,)),
            pltpu.VMEM((n_segs * CAP, 2 * NV, TILE), BF16),
            pltpu.VMEM((16 * SEGB, 2 * NV, TILE), BF16),
            pltpu.VMEM((n_segs * CAP, NV, TILE), F32),
            pltpu.VMEM((16 * SEGB, NV, TILE), F32),
        ],
        compiler_params=params(),
        cost_estimate=pl.CostEstimate(flops=48 * 2 * 3 * 2 * 256 * 256 * 256, bytes_accessed=16_000_000, transcendentals=0),
        name="cell_product",
    )(counts, slots, tiles, from_x, *from_y)


def add_parts(wanted, from_x, mine, theirs, total):
    total[...] = mine[0:SEG, :] + theirs[...]
    for d in range(from_x.shape[0]):
        for q in range(CAP):
            at = pl.ds(pl.multiple_of(wanted[d, q] * NV, NV), NV)
            total[at, :] += from_x[d, q * NV : (q + 1) * NV, :]


def gram_of(a, b):
    out = jnp.zeros((NV, NV), F32)
    for k in range(SEGB):
        out += lax.dot_general(
            a[k * NV : (k + 1) * NV, :],
            b[k * NV : (k + 1) * NV, :],
            (((1,), (1,)), ((), ())),
            precision=HIGH,
            preferred_element_type=F32,
        )
    return out


def turn_kernel(wanted, from_x, mine, theirs, seg, ride, message, total):
    add_parts(wanted, from_x, mine, theirs, total)
    pack_into(wanted, total, message)
    ride[0:SEG, :] = total[...]
    correlation = gram_of(seg, seg)
    projection = gram_of(seg, total)
    ride[SEG : SEG + RID, :] = jnp.zeros((RID, TILE), F32)
    for at, matrix in ((0, correlation), (2, projection)):
        for h in range(2):
            ride[SEG : SEG + RID, (at + h) * NV : (at + h + 1) * NV] = matrix[h * RID : (h + 1) * RID, :]


def turn(wanted, from_x, mine, theirs, seg):
    return pl.pallas_call(
        turn_kernel,
        out_shape=(
            jax.ShapeDtypeStruct((SEG + RID, TILE), F32),
            jax.ShapeDtypeStruct((from_x.shape[0], CAP * NV, TILE), F32),
        ),
        in_specs=[sspec()] + [vspec()] * 4,
        out_specs=(vspec(), vspec()),
        scratch_shapes=[pltpu.VMEM((SEG, TILE), F32)],
        compiler_params=params(),
        name="turn",
    )(wanted, from_x, mine, theirs, seg)


def solve(correlation, projection):
    m = jnp.concatenate([correlation, projection], axis=1)
    row_id = lax.broadcasted_iota(jnp.int32, m.shape, 0)
    for j in range(NV):
        row = m[j : j + 1, :] / m[j : j + 1, j : j + 1]
        m = jnp.where(row_id == j, row, m - m[:, j : j + 1] * row)
    return m[:, NV:]


def finish_kernel(wanted, from_x, mine, theirs, seg, product, residual, image, gram, total, rest):
    add_parts(wanted, from_x, mine, theirs, total)
    carried = from_x[0, CAP * NV : CAP * NV + RID, :]
    for d in range(1, from_x.shape[0]):
        carried = carried + from_x[d, CAP * NV : CAP * NV + RID, :]
    correlation, projection = (
        jnp.concatenate([carried[:, (at + h) * NV : (at + h + 1) * NV] for h in range(2)], axis=0) for at in (0, 2)
    )
    coeffs = solve(correlation, projection)
    back = coeffs.T
    for k in range(SEGB):
        at = slice(k * NV, (k + 1) * NV)
        p = product[at, :]
        r = p - jnp.dot(back, seg[at, :], precision=HIGH, preferred_element_type=F32)
        m = total[at, :] - jnp.dot(back, p, precision=HIGH, preferred_element_type=F32)
        rest[at, :] = r
        total[at, :] = m
        residual[:, k * TILE : (k + 1) * TILE] = r
        image[:, k * TILE : (k + 1) * TILE] = m
    local = gram_of(rest, total)
    for d in range(gram.shape[0]):
        gram[d] = jnp.zeros(gram.shape[1:], F32)
        for h in range(2):
            gram[d, :, h * NV : (h + 1) * NV] = local[h * RID : (h + 1) * RID, :]


def finish(wanted, from_x, mine, theirs, seg, product):
    n_segs = from_x.shape[0]
    return pl.pallas_call(
        finish_kernel,
        out_shape=(
            jax.ShapeDtypeStruct((NV, SEGB * TILE), F32),
            jax.ShapeDtypeStruct((NV, SEGB * TILE), F32),
            jax.ShapeDtypeStruct((n_segs, RID, 128), F32),
        ),
        in_specs=[sspec()] + [vspec()] * 5,
        out_specs=(vspec(),) * 3,
        scratch_shapes=[pltpu.VMEM((SEG, TILE), F32)] * 2,
        compiler_params=params(),
        name="finish",
    )(wanted, from_x, mine, theirs, seg, product)


def swap(x, axis):
    return lax.all_to_all(x, axis, 0, 0, tiled=True)


def spread(seg):
    other = lax.ppermute(seg, "row", OTHER_HALF)
    parts = [seg[:SEG], other[:SEG]]
    if seg.shape[0] > SEG:
        parts.append(seg[SEG:] + other[SEG:])
    mine = jnp.concatenate(parts, axis=0)
    near = [mine] + [lax.ppermute(mine, "row", row_shift(-step)) for step in (1, 2, 3)]
    return near + [lax.ppermute(x, "row", OTHER_CORE) for x in near]


def collect(pieces):
    met = [a + lax.ppermute(b, "row", OTHER_CORE) for a, b in zip(pieces[:4], pieces[4:])]
    both = met[0]
    for step in (1, 2, 3):
        both = both + lax.ppermute(met[step], "row", row_shift(step))
    return both, lax.ppermute(both[SEG:], "row", OTHER_HALF)


def per_device(vectors, tiles, tile_rows, tile_cols, counts):
    cell_tiles = tiles[0, 0]
    order_total = vectors.shape[1] * lax.axis_size("row") * lax.axis_size("col")
    place = lax.axis_index("row").astype(jnp.int32).reshape(1)
    seg, table, slots = prep(vectors, tile_rows, tile_cols, counts, place)
    wanted = swap(table, "col")

    from_y = spread(seg)
    from_x = swap(pack(wanted, seg), "col")
    to_x, *to_y = cell_product(counts, slots, cell_tiles, from_x, from_y, False)
    from_x = swap(to_x, "col")
    mine, theirs = collect(to_y)
    product, message = turn(wanted, from_x, mine, theirs, seg)

    from_y = spread(product)
    from_x = swap(message, "col")
    to_x, *to_y = cell_product(counts, slots, cell_tiles, from_x, from_y, True)
    from_x = swap(to_x, "col")
    mine, theirs = collect(to_y)
    residual, image, local = finish(wanted, from_x, mine, theirs, seg, product)

    part = jnp.sum(swap(local, "col"), axis=0)
    total = jnp.sum(swap(jnp.broadcast_to(part, local.shape), "row"), axis=0)
    gram = jnp.concatenate([total[:, :NV], total[:, NV : 2 * NV]], axis=0) / order_total
    return (residual, image, gram)


def solution(mesh):
    in_specs = (
        P(None, ("row", "col")),
        P("row", "col", None, None, None),
        P("row", "col", None),
        P("row", "col", None),
        P("row", "col"),
    )
    out_specs = (P(None, ("row", "col")), P(None, ("row", "col")), P())
    return jax.shard_map(
        per_device, mesh=mesh, in_specs=in_specs, out_specs=out_specs, check_vma=False
    )
```

```python
import jax
import jax.numpy as jnp
from jax import lax
from jax.experimental import pallas as pl
from jax.experimental.pallas import tpu as pltpu
from jax.sharding import Mesh
from jax.sharding import PartitionSpec as P


ROW = ("y", "zh", "core")
COL = ("x", "zl")
ROW_SIZES = (4, 2, 2)
COL_SIZES = (4, 4)
NV = 16
TILE = 256
SEGB = 6
CAP = 3
SEG = SEGB * NV
RID = 8
UNROLL = 4
F32 = jnp.float32
BF16 = jnp.bfloat16
HIGH = lax.Precision.HIGHEST
ACROSS = (((1,), (1,)), ((), ()))
MIB = 1024 * 1024


def vspec():
    return pl.BlockSpec(memory_space=pltpu.VMEM)


def sspec():
    return pl.BlockSpec(memory_space=pltpu.SMEM)


def hint(us):
    return pl.CostEstimate(flops=int(us * 1e9), bytes_accessed=0, transcendentals=0)


def params(mib):
    return pltpu.CompilerParams(vmem_limit_bytes=mib * MIB)


def turned(n, step):
    return [(i, (i + step) % n) for i in range(n)]


def prep_kernel(place, rows, cols, counts, table, slots, mark, used):
    n_segs = used.shape[0]

    def clear(b, _):
        mark[b] = -1
        return 0

    lax.fori_loop(0, n_segs * SEGB, clear, 0)

    def clear_table(s, _):
        used[s] = 0
        for q in range(CAP):
            table[s * CAP + q] = 0
        return 0

    lax.fori_loop(0, n_segs, clear_table, 0)
    my_y, my_half, my_core = place[0], place[1], place[2]

    def slot(k, _):
        b = rows[0, 0, k]
        s = b // SEGB
        old = mark[b]
        rank = jnp.where(old < 0, used[s], old)
        mark[b] = rank
        used[s] = jnp.where(old < 0, rank + 1, used[s])
        table[s * CAP + rank] = b - s * SEGB
        slots[0, k] = b
        slots[1, k] = s * CAP + rank
        g = cols[0, 0, k]
        t = g // SEGB
        step = (t // 4 + 4 - my_y) % 4
        half = (t // 2 % 2 + my_half) % 2
        core = (t % 2 + my_core) % 2
        slots[2, k] = ((core * 4 + step) * 2 + half) * SEGB + g - t * SEGB
        return 0

    lax.fori_loop(0, counts[0, 0], slot, 0)


def prep(rows, cols, counts, place):
    n_segs = 16
    return pl.pallas_call(
        prep_kernel,
        out_shape=(
            jax.ShapeDtypeStruct((n_segs * CAP,), jnp.int32),
            jax.ShapeDtypeStruct((3, rows.shape[-1]), jnp.int32),
        ),
        in_specs=[sspec()] * 4,
        out_specs=(sspec(), sspec()),
        scratch_shapes=[pltpu.SMEM((n_segs * SEGB,), jnp.int32), pltpu.SMEM((n_segs,), jnp.int32)],
        name="prep",
    )(place, rows, cols, counts)


def split(x):
    high = x.astype(BF16)
    return high, (x - high.astype(F32)).astype(BF16)


def tile_loop(count, tiles, held, sems, slot):
    def copy(k):
        return pltpu.make_async_copy(tiles.at[k], held.at[k], sems.at[k])

    def start(k, _):
        copy(k).start()
        return 0

    def one(k):
        slot(k, *split(held[k]))

    def group(g, _):
        for u in range(UNROLL):
            copy(g * UNROLL + u).wait()
        for u in range(UNROLL):
            one(g * UNROLL + u)
        return 0

    def single(k, _):
        copy(k).wait()
        one(k)
        return 0

    def run():
        whole = count // UNROLL
        lax.fori_loop(0, whole, group, 0)
        lax.fori_loop(whole * UNROLL, count, single, 0)

    lax.fori_loop(0, count, start, 0)
    return run


def put(vecs, at, block):
    high, low = split(block)
    vecs[at, 0:NV, :] = high
    vecs[at, NV : 2 * NV, :] = low


def rows_kernel(first, *refs):
    counts, slots, table, tiles = refs[:4]
    from_y = refs[4:12]
    to_x, held, sems, vecs, total = refs[12:]

    def slot(k, high, low):
        i = slots[1, k]
        v = vecs[slots[2, k]]
        a = lax.dot_general(v, high, ACROSS, preferred_element_type=F32)
        b = lax.dot_general(v[:NV], low, ACROSS, preferred_element_type=F32)
        total[i] += a[:NV] + a[NV:] + b

    run = tile_loop(counts[0, 0], tiles, held, sems, slot)
    n_segs = to_x.shape[0]
    for p in range(8):
        for h in range(2):
            for b in range(SEGB):
                at = (p * 2 + h) * SEGB + b
                if first:
                    put(vecs, at, from_y[p][h, :, b * TILE : (b + 1) * TILE])
                else:
                    put(vecs, at, from_y[p][(h * SEGB + b) * NV : (h * SEGB + b + 1) * NV, :])
    total[...] = jnp.zeros(total.shape, F32)
    run()
    if not first:
        carried = from_y[0][2 * SEG : 2 * SEG + RID, :]
        for p in range(1, 8):
            carried = carried + from_y[p][2 * SEG : 2 * SEG + RID, :]
    for s in range(n_segs):
        for q in range(CAP):
            to_x[s, q * NV : (q + 1) * NV, :] = total[s * CAP + q]
        if first:
            row_id = lax.broadcasted_iota(jnp.int32, (RID, TILE), 0)
            carried = jnp.zeros((RID, TILE), jnp.int32)
            for q in range(CAP):
                carried = jnp.where(row_id == q, table[s * CAP + q], carried)
            carried = carried.astype(F32)
        to_x[s, CAP * NV : CAP * NV + RID, :] = carried


def cols_kernel(first, *refs):
    counts, slots, tiles, from_x = refs[:4]
    to_y = refs[4:12]
    held, sems, vecs, total = refs[12:]

    def slot(k, high, low):
        j = slots[2, k]
        v = vecs[slots[0 if first else 1, k]]
        a = jnp.dot(v, high, preferred_element_type=F32)
        b = jnp.dot(v[:NV], low, preferred_element_type=F32)
        total[j] += a[:NV] + a[NV:] + b

    run = tile_loop(counts[0, 0], tiles, held, sems, slot)
    in_seg = SEGB if first else CAP
    for s in range(from_x.shape[0]):
        for q in range(in_seg):
            if first:
                put(vecs, s * in_seg + q, from_x[s, :, q * TILE : (q + 1) * TILE])
            else:
                put(vecs, s * in_seg + q, from_x[s, q * NV : (q + 1) * NV, :])
    total[...] = jnp.zeros(total.shape, F32)
    run()
    for p in range(8):
        for b in range(2 * SEGB):
            to_y[p][b * NV : (b + 1) * NV, :] = total[p * 2 * SEGB + b]


def tile_scratch(tiles):
    return [pltpu.VMEM(tiles.shape, F32), pltpu.SemaphoreType.DMA(tiles.shape[:1])]


def rows_product(counts, slots, table, tiles, from_y, first):
    def kernel(*refs):
        rows_kernel(first, *refs)

    return pl.pallas_call(
        kernel,
        out_shape=jax.ShapeDtypeStruct((16, CAP * NV + RID, TILE), F32),
        in_specs=[sspec()] * 3 + [pl.BlockSpec(memory_space=pltpu.HBM)] + [vspec()] * 8,
        out_specs=vspec(),
        scratch_shapes=tile_scratch(tiles)
        + [pltpu.VMEM((16 * SEGB, 2 * NV, TILE), BF16), pltpu.VMEM((16 * CAP, NV, TILE), F32)],
        compiler_params=params(24),
        cost_estimate=hint(10 if first else 5),
        name="rows_product",
    )(counts, slots, table, tiles, *from_y)


def cols_product(counts, slots, tiles, from_x, first):
    def kernel(*refs):
        cols_kernel(first, *refs)

    return pl.pallas_call(
        kernel,
        out_shape=(jax.ShapeDtypeStruct((2 * SEG, TILE), F32),) * 8,
        in_specs=[sspec()] * 2 + [pl.BlockSpec(memory_space=pltpu.HBM), vspec()],
        out_specs=(vspec(),) * 8,
        scratch_shapes=tile_scratch(tiles)
        + [
            pltpu.VMEM((16 * (SEGB if first else CAP), 2 * NV, TILE), BF16),
            pltpu.VMEM((16 * SEGB, NV, TILE), F32),
        ],
        compiler_params=params(24),
        cost_estimate=hint(5),
        name="cols_product",
    )(counts, slots, tiles, from_x)


def add_terms(wanted, from_x, total):
    for b in range(SEGB):
        at = slice(b * NV, (b + 1) * NV)
        block = total[at, :]
        for d in range(from_x.shape[0]):
            for q in range(CAP):
                term = from_x[d, q * NV : (q + 1) * NV, :]
                block = block + jnp.where(wanted[d, q : q + 1, :] == b, term, 0.0)
        total[at, :] = block


def near_kernel(from_x, wanted, total):
    total[...] = jnp.zeros(total.shape, F32)
    wanted[...] = from_x[:, CAP * NV : CAP * NV + RID, :]
    add_terms(wanted, from_x, total)


def near(from_x):
    return pl.pallas_call(
        near_kernel,
        out_shape=(
            jax.ShapeDtypeStruct((from_x.shape[0], RID, TILE), F32),
            jax.ShapeDtypeStruct((SEG, TILE), F32),
        ),
        in_specs=[vspec()],
        out_specs=(vspec(), vspec()),
        compiler_params=params(8),
        name="near",
    )(from_x)


def turn_kernel(wanted, near_mine, far_mine, far_theirs, product, message):
    for b in range(SEGB):
        at = slice(b * NV, (b + 1) * NV)
        product[at, :] = near_mine[at, :] + (far_mine[at, :] + far_theirs[at, :])
    for d in range(message.shape[0]):
        for q in range(CAP):
            want = wanted[d, q : q + 1, :]
            block = jnp.zeros((NV, TILE), F32)
            for b in range(SEGB):
                block = jnp.where(want == b, product[b * NV : (b + 1) * NV, :], block)
            message[d, q * NV : (q + 1) * NV, :] = block


def turn(wanted, near_mine, far_mine, far_theirs):
    return pl.pallas_call(
        turn_kernel,
        out_shape=(
            jax.ShapeDtypeStruct((SEG, TILE), F32),
            jax.ShapeDtypeStruct((wanted.shape[0], CAP * NV, TILE), F32),
        ),
        in_specs=[vspec()] * 4,
        out_specs=(vspec(), vspec()),
        compiler_params=params(8),
        name="turn",
    )(wanted, near_mine, far_mine, far_theirs)


def cross(a, b):
    return lax.dot_general(a, b, ACROSS, precision=HIGH, preferred_element_type=F32)


def fan_kernel(table, slots, mine, theirs, pair, correlation):
    pair[0] = mine[...]
    pair[1] = theirs[...]
    correlation[...] = cross(mine[...], mine[...]) + cross(theirs[...], theirs[...])


def fan(table, slots, mine, theirs):
    return pl.pallas_call(
        fan_kernel,
        out_shape=(
            jax.ShapeDtypeStruct((2,) + mine.shape, F32),
            jax.ShapeDtypeStruct((NV, NV), F32),
        ),
        in_specs=[sspec()] * 2 + [vspec()] * 2,
        out_specs=(vspec(),) * 2,
        compiler_params=params(8),
        cost_estimate=hint(20),
        name="fan",
    )(table, slots, mine, theirs)


def load_kernel(product, other, mine, theirs, correlation, ride):
    ride[0:SEG, :] = product[...]
    ride[SEG : 2 * SEG, :] = other[...]
    projection = jnp.zeros((NV, NV), F32)
    for h, vectors in enumerate((mine, theirs)):
        for b in range(SEGB):
            at = (h * SEGB + b) * NV
            projection += cross(vectors[:, b * TILE : (b + 1) * TILE], ride[at : at + NV, :])
    ride[2 * SEG : 2 * SEG + RID, :] = jnp.zeros((RID, TILE), F32)
    for at, matrix in ((0, correlation[...]), (2, projection)):
        for h in range(2):
            ride[2 * SEG : 2 * SEG + RID, (at + h) * NV : (at + h + 1) * NV] = matrix[h * RID : (h + 1) * RID, :]


def load(product, other, mine, theirs, correlation):
    return pl.pallas_call(
        load_kernel,
        out_shape=jax.ShapeDtypeStruct((2 * SEG + RID, TILE), F32),
        in_specs=[vspec()] * 5,
        out_specs=vspec(),
        compiler_params=params(4),
        cost_estimate=hint(50),
        name="load",
    )(product, other, mine, theirs, correlation)


def solve(correlation, projection):
    m = jnp.concatenate([correlation, projection], axis=1)
    row_id = lax.broadcasted_iota(jnp.int32, m.shape, 0)
    for j in range(NV):
        row = m[j : j + 1, :] / m[j : j + 1, j : j + 1]
        m = jnp.where(row_id == j, row, m - m[:, j : j + 1] * row)
    return m[:, NV:]


def finish_kernel(wanted, from_x, both, mine, theirs, pair, residual, image, gram, total):
    total[...] = both[0:SEG, :]
    add_terms(wanted, from_x, total)
    carried = from_x[0, CAP * NV : CAP * NV + RID, :]
    for d in range(1, from_x.shape[0]):
        carried = carried + from_x[d, CAP * NV : CAP * NV + RID, :]
    correlation, projection = (
        jnp.concatenate([carried[:, (at + h) * NV : (at + h + 1) * NV] for h in range(2)], axis=0) for at in (0, 2)
    )
    coeffs = solve(correlation, projection)
    back = coeffs.T
    local = jnp.zeros((NV, NV), F32)
    for b in range(SEGB):
        at = slice(b * NV, (b + 1) * NV)
        other = slice(SEG + b * NV, SEG + (b + 1) * NV)
        cols = slice(b * TILE, (b + 1) * TILE)
        p = pair[at, :]
        r = p - jnp.dot(back, mine[:, cols], precision=HIGH, preferred_element_type=F32)
        m = total[at, :] - jnp.dot(back, p, precision=HIGH, preferred_element_type=F32)
        residual[:, cols] = r
        image[:, cols] = m
        r_other = pair[other, :] - jnp.dot(back, theirs[:, cols], precision=HIGH, preferred_element_type=F32)
        local += cross(r, m) + cross(r_other, both[other, :])
    for d in range(gram.shape[0]):
        gram[d] = jnp.zeros(gram.shape[1:], F32)
        for h in range(2):
            gram[d, :, h * NV : (h + 1) * NV] = local[h * RID : (h + 1) * RID, :]


def finish(wanted, from_x, both, mine, theirs, pair):
    return pl.pallas_call(
        finish_kernel,
        out_shape=(
            jax.ShapeDtypeStruct(mine.shape, F32),
            jax.ShapeDtypeStruct(mine.shape, F32),
            jax.ShapeDtypeStruct((16, RID, 128), F32),
        ),
        in_specs=[vspec()] * 6,
        out_specs=(vspec(),) * 3,
        scratch_shapes=[pltpu.VMEM((SEG, TILE), F32)],
        compiler_params=params(8),
        name="finish",
    )(wanted, from_x, both, mine, theirs, pair)


def last_kernel(part, far, image):
    for b in range(SEGB):
        cols = slice(b * TILE, (b + 1) * TILE)
        image[:, cols] = part[:, cols] + far[b * NV : (b + 1) * NV, :]


def last(part, far):
    return pl.pallas_call(
        last_kernel,
        out_shape=jax.ShapeDtypeStruct(part.shape, F32),
        in_specs=[vspec()] * 2,
        out_specs=vspec(),
        compiler_params=params(4),
        name="last",
    )(part, far)


def swap(x, axis):
    return lax.all_to_all(x, axis, 0, 0, tiled=True)


def other_half(x):
    return lax.ppermute(x, "zh", turned(2, 1))


def other_core(x):
    return lax.ppermute(x, "core", turned(2, 1))


def spread(mine):
    pieces = [mine] + [lax.ppermute(mine, "y", turned(4, -step)) for step in (1, 2, 3)]
    return pieces + [other_core(x) for x in pieces]


def collect(pieces):
    met = [a + other_core(b) for a, b in zip(pieces[:4], pieces[4:])]
    both = met[0]
    for step in (1, 2, 3):
        both = both + lax.ppermute(met[step], "y", turned(4, step))
    return both


def per_device(vectors, tiles, tile_rows, tile_cols, counts):
    cell_tiles = pltpu.with_memory_space_constraint(tiles[0, 0], pltpu.HBM)
    order_total = vectors.shape[1] * lax.axis_size(ROW) * lax.axis_size(COL)
    place = jnp.stack([lax.axis_index(name).astype(jnp.int32) for name in ROW])
    table, slots = prep(tile_rows, tile_cols, counts, place)

    theirs = other_half(vectors)
    both, correlation = fan(table, slots, vectors, theirs)
    from_y = spread(both)
    line = swap(jnp.broadcast_to(vectors, (4,) + vectors.shape), "zl")
    from_x = swap(jnp.broadcast_to(line, (4,) + line.shape), "x").reshape((16,) + vectors.shape)
    to_x = rows_product(counts, slots, table, cell_tiles, from_y, True)
    to_y = cols_product(counts, slots, cell_tiles, from_x, True)
    from_x = swap(to_x, COL)
    both = collect(to_y)
    far = other_half(both[SEG:])
    wanted, mine = near(from_x)
    product, message = turn(wanted, mine, both, far)

    from_x = swap(message, COL)
    pair = load(product, other_half(product), vectors, theirs, correlation)
    from_y = spread(pair)
    to_x = rows_product(counts, slots, table, cell_tiles, from_y, False)
    to_y = cols_product(counts, slots, cell_tiles, from_x, False)
    from_x = swap(to_x, COL)
    both = collect(to_y)
    residual, part, local = finish(wanted, from_x, both, vectors, theirs, pair)
    image = last(part, other_half(both[SEG:]))

    some = jnp.sum(swap(local, ("zh", "zl", "core")), axis=0)
    total = jnp.sum(swap(jnp.broadcast_to(some, local.shape), ("x", "y")), axis=0)
    gram = jnp.concatenate([total[:, :NV], total[:, NV : 2 * NV]], axis=0) / order_total
    return (residual, image, gram)


def solution(mesh):
    fine = Mesh(mesh.devices.reshape(ROW_SIZES + COL_SIZES), ROW + COL)
    in_specs = (
        P(None, ROW + COL),
        P(ROW, COL, None, None, None),
        P(ROW, COL, None),
        P(ROW, COL, None),
        P(ROW, COL),
    )
    out_specs = (P(None, ROW + COL), P(None, ROW + COL), P())
    return jax.shard_map(
        per_device, mesh=fine, in_specs=in_specs, out_specs=out_specs, check_vma=False
    )
```

```python
import jax
import jax.numpy as jnp
from jax import lax
from jax.experimental import pallas as pl
from jax.experimental.pallas import tpu as pltpu
from jax.sharding import Mesh
from jax.sharding import PartitionSpec as P


ROW = ("y", "zh", "core")
COL = ("x", "zl")
ROW_SIZES = (4, 2, 2)
COL_SIZES = (4, 4)
NV = 16
TILE = 256
SEGB = 6
CAP = 3
SEG = SEGB * NV
RID = 8
MAXT = 48
COUNT = 2 * MAXT
PLACE = COUNT + 1
UNROLL = 4
F32 = jnp.float32
BF16 = jnp.bfloat16
HIGH = lax.Precision.HIGHEST
ACROSS = (((1,), (1,)), ((), ()))
MIB = 1024 * 1024


def vspec():
    return pl.BlockSpec(memory_space=pltpu.VMEM)


def sspec():
    return pl.BlockSpec(memory_space=pltpu.SMEM)


def hint(us):
    return pl.CostEstimate(flops=int(us * 1e9), bytes_accessed=0, transcendentals=0)


def params(mib):
    return pltpu.CompilerParams(vmem_limit_bytes=mib * MIB)


def turned(n, step):
    return [(i, (i + step) % n) for i in range(n)]


def prep_kernel(facts, slots, ids, table, mark, used):
    n_segs = used.shape[0]

    def clear(b, _):
        mark[b] = -1
        return 0

    lax.fori_loop(0, n_segs * SEGB, clear, 0)

    def clear_table(s, _):
        used[s] = 0
        for q in range(CAP):
            table[s * CAP + q] = 0
        return 0

    lax.fori_loop(0, n_segs, clear_table, 0)
    count, my_y, my_half, my_core = facts[COUNT], facts[PLACE], facts[PLACE + 1], facts[PLACE + 2]

    def slot(k, _):
        b = facts[k]
        s = b // SEGB
        old = mark[b]
        rank = jnp.where(old < 0, used[s], old)
        mark[b] = rank
        used[s] = jnp.where(old < 0, rank + 1, used[s])
        table[s * CAP + rank] = b - s * SEGB
        slots[0, k] = s * CAP + rank
        g = facts[MAXT + k]
        t = g // SEGB
        step = (t // 4 + 4 - my_y) % 4
        half = (t // 2 % 2 + my_half) % 2
        core = (t % 2 + my_core) % 2
        slots[1, k] = ((core * 4 + step) * 2 + half) * SEGB + g - t * SEGB
        return 0

    lax.fori_loop(0, count, slot, 0)
    row_id = lax.broadcasted_iota(jnp.int32, (RID, TILE), 0)

    for s in range(n_segs):
        out = jnp.zeros((RID, TILE), jnp.int32)
        for q in range(CAP):
            out = jnp.where(row_id == q, table[s * CAP + q], out)
        ids[s] = out.astype(F32)


def prep(facts):
    n_segs = 16
    return pl.pallas_call(
        prep_kernel,
        out_shape=(
            jax.ShapeDtypeStruct((2, MAXT), jnp.int32),
            jax.ShapeDtypeStruct((n_segs, RID, TILE), F32),
        ),
        in_specs=[sspec()],
        out_specs=(sspec(), vspec()),
        scratch_shapes=[
            pltpu.SMEM((n_segs * CAP,), jnp.int32),
            pltpu.SMEM((n_segs * SEGB,), jnp.int32),
            pltpu.SMEM((n_segs,), jnp.int32),
        ],
        compiler_params=params(4),
        cost_estimate=hint(2),
        name="prep",
    )(facts)


def pack_kernel(facts, line, *refs):
    asked, message = refs[:4], refs[4]
    for k in range(4):
        to = (facts[PLACE + 3] + 4 - k) % 4
        for z in range(4):
            for q in range(CAP):
                want = asked[k][facts[PLACE + 3] * 4 + z, q : q + 1, :]
                block = jnp.zeros((NV, TILE), F32)
                for b in range(SEGB):
                    block = jnp.where(want == b, line[z, :, b * TILE : (b + 1) * TILE], block)
                message[to, z, q * NV : (q + 1) * NV, :] = block


def pack(facts, line, asked):
    return pl.pallas_call(
        pack_kernel,
        out_shape=jax.ShapeDtypeStruct((4, 4, CAP * NV, TILE), F32),
        in_specs=[sspec()] + [vspec()] * 5,
        out_specs=vspec(),
        compiler_params=params(8),
        cost_estimate=hint(1),
        name="pack",
    )(facts, line, *asked)


def split(x):
    high = x.astype(BF16)
    return high, (x - high.astype(F32)).astype(BF16)


def tile_loop(count, tiles, held, sems, slot):
    def copy(k):
        return pltpu.make_async_copy(tiles.at[k], held.at[k], sems.at[k])

    def start(k, _):
        copy(k).start()
        return 0

    def one(k):
        slot(k, *split(held[k]))

    def group(g, _):
        for u in range(UNROLL):
            copy(g * UNROLL + u).wait()
        for u in range(UNROLL):
            one(g * UNROLL + u)
        return 0

    def single(k, _):
        copy(k).wait()
        one(k)
        return 0

    def run():
        whole = count // UNROLL
        lax.fori_loop(0, whole, group, 0)
        lax.fori_loop(whole * UNROLL, count, single, 0)

    lax.fori_loop(0, count, start, 0)
    return run


def put(vecs, at, block):
    high, low = split(block)
    vecs[at, 0:NV, :] = high
    vecs[at, NV : 2 * NV, :] = low


def rows_kernel(first, *refs):
    facts, slots, ids, tiles = refs[:4]
    from_y = refs[4:12]
    to_x, held, sems, vecs, total = refs[12:]

    def slot(k, high, low):
        i = slots[0, k]
        v = vecs[slots[1, k]]
        a = lax.dot_general(v, high, ACROSS, preferred_element_type=F32)
        b = lax.dot_general(v[:NV], low, ACROSS, preferred_element_type=F32)
        total[i] += a[:NV] + a[NV:] + b

    run = tile_loop(facts[COUNT], tiles, held, sems, slot)
    n_segs = to_x.shape[0]
    for p in range(8):
        for h in range(2):
            for b in range(SEGB):
                at = (p * 2 + h) * SEGB + b
                if first:
                    put(vecs, at, from_y[p][h, :, b * TILE : (b + 1) * TILE])
                else:
                    put(vecs, at, from_y[p][(h * SEGB + b) * NV : (h * SEGB + b + 1) * NV, :])
    total[...] = jnp.zeros(total.shape, F32)
    run()
    if not first:
        carried = from_y[0][2 * SEG : 2 * SEG + RID, :]
        for p in range(1, 8):
            carried = carried + from_y[p][2 * SEG : 2 * SEG + RID, :]
    for s in range(n_segs):
        for q in range(CAP):
            to_x[s, q * NV : (q + 1) * NV, :] = total[s * CAP + q]
        if first:
            carried = ids[s]
        to_x[s, CAP * NV : CAP * NV + RID, :] = carried


def cols_kernel(*refs):
    facts, slots, tiles, from_x = refs[:4]
    to_y = refs[4:12]
    held, sems, vecs, total = refs[12:]

    def slot(k, high, low):
        j = slots[1, k]
        v = vecs[slots[0, k]]
        a = jnp.dot(v, high, preferred_element_type=F32)
        b = jnp.dot(v[:NV], low, preferred_element_type=F32)
        total[j] += a[:NV] + a[NV:] + b

    run = tile_loop(facts[COUNT], tiles, held, sems, slot)
    for s in range(from_x.shape[0]):
        for q in range(CAP):
            put(vecs, s * CAP + q, from_x[s, q * NV : (q + 1) * NV, :])
    total[...] = jnp.zeros(total.shape, F32)
    run()
    for p in range(8):
        for b in range(2 * SEGB):
            to_y[p][b * NV : (b + 1) * NV, :] = total[p * 2 * SEGB + b]


def tile_scratch(tiles):
    return [pltpu.VMEM(tiles.shape, F32), pltpu.SemaphoreType.DMA(tiles.shape[:1])]


def rows_product(facts, slots, ids, tiles, from_y, first):
    def kernel(*refs):
        rows_kernel(first, *refs)

    return pl.pallas_call(
        kernel,
        out_shape=jax.ShapeDtypeStruct((16, CAP * NV + RID, TILE), F32),
        in_specs=[sspec()] * 2 + [vspec(), pl.BlockSpec(memory_space=pltpu.HBM)] + [vspec()] * 8,
        out_specs=vspec(),
        scratch_shapes=tile_scratch(tiles)
        + [pltpu.VMEM((16 * SEGB, 2 * NV, TILE), BF16), pltpu.VMEM((16 * CAP, NV, TILE), F32)],
        compiler_params=params(24),
        cost_estimate=hint(4 if first else 5),
        name="rows_product",
    )(facts, slots, ids, tiles, *from_y)


def cols_product(facts, slots, tiles, from_x):
    return pl.pallas_call(
        cols_kernel,
        out_shape=(jax.ShapeDtypeStruct((2 * SEG, TILE), F32),) * 8,
        in_specs=[sspec()] * 2 + [pl.BlockSpec(memory_space=pltpu.HBM), vspec()],
        out_specs=(vspec(),) * 8,
        scratch_shapes=tile_scratch(tiles)
        + [
            pltpu.VMEM((16 * CAP, 2 * NV, TILE), BF16),
            pltpu.VMEM((16 * SEGB, NV, TILE), F32),
        ],
        compiler_params=params(24),
        cost_estimate=hint(5),
        name="cols_product",
    )(facts, slots, tiles, from_x)


def add_terms(wanted, from_x, total):
    for b in range(SEGB):
        at = slice(b * NV, (b + 1) * NV)
        block = total[at, :]
        for d in range(from_x.shape[0]):
            for q in range(CAP):
                term = from_x[d, q * NV : (q + 1) * NV, :]
                block = block + jnp.where(wanted[d, q : q + 1, :] == b, term, 0.0)
        total[at, :] = block


def near_kernel(from_x, wanted, total):
    total[...] = jnp.zeros(total.shape, F32)
    wanted[...] = from_x[:, CAP * NV : CAP * NV + RID, :]
    add_terms(wanted, from_x, total)


def near(from_x):
    return pl.pallas_call(
        near_kernel,
        out_shape=(
            jax.ShapeDtypeStruct((from_x.shape[0], RID, TILE), F32),
            jax.ShapeDtypeStruct((SEG, TILE), F32),
        ),
        in_specs=[vspec()],
        out_specs=(vspec(), vspec()),
        compiler_params=params(8),
        name="near",
    )(from_x)


def turn_kernel(wanted, near_mine, far_mine, far_theirs, product, message):
    for b in range(SEGB):
        at = slice(b * NV, (b + 1) * NV)
        product[at, :] = near_mine[at, :] + (far_mine[at, :] + far_theirs[at, :])
    for d in range(message.shape[0]):
        for q in range(CAP):
            want = wanted[d, q : q + 1, :]
            block = jnp.zeros((NV, TILE), F32)
            for b in range(SEGB):
                block = jnp.where(want == b, product[b * NV : (b + 1) * NV, :], block)
            message[d, q * NV : (q + 1) * NV, :] = block


def turn(wanted, near_mine, far_mine, far_theirs):
    return pl.pallas_call(
        turn_kernel,
        out_shape=(
            jax.ShapeDtypeStruct((SEG, TILE), F32),
            jax.ShapeDtypeStruct((wanted.shape[0], CAP * NV, TILE), F32),
        ),
        in_specs=[vspec()] * 4,
        out_specs=(vspec(), vspec()),
        compiler_params=params(8),
        name="turn",
    )(wanted, near_mine, far_mine, far_theirs)


def cross(a, b):
    return lax.dot_general(a, b, ACROSS, precision=HIGH, preferred_element_type=F32)


def fan_kernel(mine, theirs, pair, correlation):
    pair[0] = mine[...]
    pair[1] = theirs[...]
    correlation[...] = cross(mine[...], mine[...]) + cross(theirs[...], theirs[...])


def fan(mine, theirs):
    return pl.pallas_call(
        fan_kernel,
        out_shape=(
            jax.ShapeDtypeStruct((2,) + mine.shape, F32),
            jax.ShapeDtypeStruct((NV, NV), F32),
        ),
        in_specs=[vspec()] * 2,
        out_specs=(vspec(),) * 2,
        compiler_params=params(8),
        cost_estimate=hint(5),
        name="fan",
    )(mine, theirs)


def load_kernel(product, other, mine, theirs, correlation, ride):
    ride[0:SEG, :] = product[...]
    ride[SEG : 2 * SEG, :] = other[...]
    projection = jnp.zeros((NV, NV), F32)
    for h, vectors in enumerate((mine, theirs)):
        for b in range(SEGB):
            at = (h * SEGB + b) * NV
            projection += cross(vectors[:, b * TILE : (b + 1) * TILE], ride[at : at + NV, :])
    ride[2 * SEG : 2 * SEG + RID, :] = jnp.zeros((RID, TILE), F32)
    for at, matrix in ((0, correlation[...]), (2, projection)):
        for h in range(2):
            ride[2 * SEG : 2 * SEG + RID, (at + h) * NV : (at + h + 1) * NV] = matrix[h * RID : (h + 1) * RID, :]


def load(product, other, mine, theirs, correlation):
    return pl.pallas_call(
        load_kernel,
        out_shape=jax.ShapeDtypeStruct((2 * SEG + RID, TILE), F32),
        in_specs=[vspec()] * 5,
        out_specs=vspec(),
        compiler_params=params(4),
        cost_estimate=hint(50),
        name="load",
    )(product, other, mine, theirs, correlation)


def solve(correlation, projection):
    m = jnp.concatenate([correlation, projection], axis=1)
    row_id = lax.broadcasted_iota(jnp.int32, m.shape, 0)
    for j in range(NV):
        row = m[j : j + 1, :] / m[j : j + 1, j : j + 1]
        m = jnp.where(row_id == j, row, m - m[:, j : j + 1] * row)
    return m[:, NV:]


def thirds(x):
    high = x.astype(BF16)
    rest = x - high.astype(F32)
    middle = rest.astype(BF16)
    return high, middle, (rest - middle.astype(F32)).astype(BF16)


def stack_left(x):
    a, b, c = thirds(x)
    return jnp.concatenate([a, a, b, a, b, c], axis=1)


def times(left, x):
    a, b, c = thirds(x)
    right = jnp.concatenate([a, b, a, c, b, a], axis=0)
    return jnp.dot(left, right, preferred_element_type=F32)


def finish_kernel(wanted, from_x, both, mine, theirs, pair, residual, image, gram, total):
    total[...] = both[0:SEG, :]
    add_terms(wanted, from_x, total)
    carried = from_x[0, CAP * NV : CAP * NV + RID, :]
    for d in range(1, from_x.shape[0]):
        carried = carried + from_x[d, CAP * NV : CAP * NV + RID, :]
    correlation, projection = (
        jnp.concatenate([carried[:, (at + h) * NV : (at + h + 1) * NV] for h in range(2)], axis=0) for at in (0, 2)
    )
    coeffs = solve(correlation, projection)
    back = stack_left(coeffs.T)
    local = jnp.zeros((NV, NV), F32)
    for b in range(SEGB):
        at = slice(b * NV, (b + 1) * NV)
        other = slice(SEG + b * NV, SEG + (b + 1) * NV)
        cols = slice(b * TILE, (b + 1) * TILE)
        p = pair[at, :]
        r = p - times(back, mine[:, cols])
        m = total[at, :] - times(back, p)
        residual[:, cols] = r
        image[:, cols] = m
        r_other = pair[other, :] - times(back, theirs[:, cols])
        local += cross(r, m) + cross(r_other, both[other, :])
    for d in range(gram.shape[0]):
        gram[d] = jnp.zeros(gram.shape[1:], F32)
        for h in range(2):
            gram[d, :, h * NV : (h + 1) * NV] = local[h * RID : (h + 1) * RID, :]


def finish(wanted, from_x, both, mine, theirs, pair):
    return pl.pallas_call(
        finish_kernel,
        out_shape=(
            jax.ShapeDtypeStruct(mine.shape, F32),
            jax.ShapeDtypeStruct(mine.shape, F32),
            jax.ShapeDtypeStruct((16, RID, 128), F32),
        ),
        in_specs=[vspec()] * 6,
        out_specs=(vspec(),) * 3,
        scratch_shapes=[pltpu.VMEM((SEG, TILE), F32)],
        compiler_params=params(8),
        name="finish",
    )(wanted, from_x, both, mine, theirs, pair)


def last_kernel(part, far, image):
    for b in range(SEGB):
        cols = slice(b * TILE, (b + 1) * TILE)
        image[:, cols] = part[:, cols] + far[b * NV : (b + 1) * NV, :]


def last(part, far):
    return pl.pallas_call(
        last_kernel,
        out_shape=jax.ShapeDtypeStruct(part.shape, F32),
        in_specs=[vspec()] * 2,
        out_specs=vspec(),
        compiler_params=params(4),
        name="last",
    )(part, far)


def in_hbm(x):
    return pltpu.with_memory_space_constraint(x, pltpu.HBM)


def swap(x, axis):
    return lax.all_to_all(x, axis, 0, 0, tiled=True)


def other_half(x):
    return lax.ppermute(x, "zh", turned(2, 1))


def other_core(x):
    return lax.ppermute(x, "core", turned(2, 1))


def spread(mine):
    pieces = [mine] + [lax.ppermute(mine, "y", turned(4, -step)) for step in (1, 2, 3)]
    return pieces + [other_core(x) for x in pieces]


def collect(pieces):
    met = [a + other_core(b) for a, b in zip(pieces[:4], pieces[4:])]
    both = met[0]
    for step in (1, 2, 3):
        both = both + lax.ppermute(met[step], "y", turned(4, step))
    return both


def per_device(vectors, tiles, tile_rows, tile_cols, counts):
    cell_tiles = in_hbm(tiles[0, 0])
    order_total = vectors.shape[1] * lax.axis_size(ROW) * lax.axis_size(COL)
    place = jnp.stack([lax.axis_index(name).astype(jnp.int32) for name in ROW + ("x",)])
    facts = jnp.concatenate([tile_rows.reshape(MAXT), tile_cols.reshape(MAXT), counts.reshape(1), place])
    slots, ids = prep(facts)
    asked = [ids] + [lax.ppermute(ids, "x", turned(4, k)) for k in (1, 2, 3)]

    theirs = other_half(vectors)
    both, correlation = fan(in_hbm(vectors), theirs)
    from_y = spread(both)
    line = swap(jnp.broadcast_to(vectors, (4,) + vectors.shape), "zl")
    from_x = swap(pack(facts, line, asked), "x").reshape(16, CAP * NV, TILE)
    to_x = rows_product(facts, slots, ids, cell_tiles, from_y, True)
    to_y = cols_product(facts, slots, cell_tiles, from_x)
    from_x = swap(to_x, COL)
    both = collect(to_y)
    far = other_half(both[SEG:])
    wanted, mine = near(from_x)
    product, message = turn(wanted, mine, both, far)

    from_x = swap(message, COL)
    pair = load(product, other_half(product), vectors, theirs, correlation)
    from_y = spread(pair)
    to_x = rows_product(facts, slots, ids, cell_tiles, from_y, False)
    to_y = cols_product(facts, slots, cell_tiles, from_x)
    from_x = swap(to_x, COL)
    both = collect(to_y)
    residual, part, local = finish(wanted, from_x, both, vectors, theirs, pair)
    image = last(part, other_half(both[SEG:]))

    some = jnp.sum(swap(local, ("zh", "zl", "core")), axis=0)
    total = jnp.sum(swap(jnp.broadcast_to(some, local.shape), ("x", "y")), axis=0)
    gram = jnp.concatenate([total[:, :NV], total[:, NV : 2 * NV]], axis=0) / order_total
    return (residual, image, gram)


def solution(mesh):
    fine = Mesh(mesh.devices.reshape(ROW_SIZES + COL_SIZES), ROW + COL)
    in_specs = (
        P(None, ROW + COL),
        P(ROW, COL, None, None, None),
        P(ROW, COL, None),
        P(ROW, COL, None),
        P(ROW, COL),
    )
    out_specs = (P(None, ROW + COL), P(None, ROW + COL), P())
    return jax.shard_map(
        per_device, mesh=fine, in_specs=in_specs, out_specs=out_specs, check_vma=False
    )
```

```python
import jax
import jax.numpy as jnp
from jax import lax
from jax.experimental import pallas as pl
from jax.experimental.pallas import tpu as pltpu
from jax.sharding import Mesh
from jax.sharding import PartitionSpec as P


ROW = ("y", "zh", "core")
COL = ("x", "zl")
ROW_SIZES = (4, 2, 2)
COL_SIZES = (4, 4)
NV = 16
TILE = 256
SEGB = 6
CAP = 3
SEG = SEGB * NV
RID = 8
MAXT = 48
COUNT = 2 * MAXT
PLACE = COUNT + 1
UNROLL = 8
F32 = jnp.float32
BF16 = jnp.bfloat16
HIGH = lax.Precision.HIGHEST
ACROSS = (((1,), (1,)), ((), ()))
MIB = 1024 * 1024


def vspec():
    return pl.BlockSpec(memory_space=pltpu.VMEM)


def sspec():
    return pl.BlockSpec(memory_space=pltpu.SMEM)


def hint(us):
    return pl.CostEstimate(flops=int(us * 1e9), bytes_accessed=0, transcendentals=0)


def params(mib):
    return pltpu.CompilerParams(vmem_limit_bytes=mib * MIB)


def turned(n, step):
    return [(i, (i + step) % n) for i in range(n)]


def prep_kernel(facts, slots, ids, table, mark, used):
    n_segs = used.shape[0]

    def clear(b, _):
        mark[b] = -1
        return 0

    lax.fori_loop(0, n_segs * SEGB, clear, 0)

    def clear_table(s, _):
        used[s] = 0
        for q in range(CAP):
            table[s * CAP + q] = 0
        return 0

    lax.fori_loop(0, n_segs, clear_table, 0)
    count, my_y, my_half, my_core = facts[COUNT], facts[PLACE], facts[PLACE + 1], facts[PLACE + 2]

    def slot(k, _):
        b = facts[k]
        s = b // SEGB
        old = mark[b]
        rank = jnp.where(old < 0, used[s], old)
        mark[b] = rank
        used[s] = jnp.where(old < 0, rank + 1, used[s])
        table[s * CAP + rank] = b - s * SEGB
        slots[0, k] = s * CAP + rank
        g = facts[MAXT + k]
        t = g // SEGB
        step = (t // 4 + 4 - my_y) % 4
        half = (t // 2 % 2 + my_half) % 2
        core = (t % 2 + my_core) % 2
        slots[1, k] = ((core * 4 + step) * 2 + half) * SEGB + g - t * SEGB
        return 0

    lax.fori_loop(0, count, slot, 0)
    row_id = lax.broadcasted_iota(jnp.int32, (RID, TILE), 0)

    for s in range(n_segs):
        out = jnp.zeros((RID, TILE), jnp.int32)
        for q in range(CAP):
            out = jnp.where(row_id == q, table[s * CAP + q], out)
        ids[s] = out.astype(F32)


def prep(facts):
    n_segs = 16
    return pl.pallas_call(
        prep_kernel,
        out_shape=(
            jax.ShapeDtypeStruct((2, MAXT), jnp.int32),
            jax.ShapeDtypeStruct((n_segs, RID, TILE), F32),
        ),
        in_specs=[sspec()],
        out_specs=(sspec(), vspec()),
        scratch_shapes=[
            pltpu.SMEM((n_segs * CAP,), jnp.int32),
            pltpu.SMEM((n_segs * SEGB,), jnp.int32),
            pltpu.SMEM((n_segs,), jnp.int32),
        ],
        compiler_params=params(4),
        cost_estimate=hint(2),
        name="prep",
    )(facts)


def pack_kernel(facts, line, *refs):
    asked, message = refs[:4], refs[4]
    for k in range(4):
        to = (facts[PLACE + 3] + 4 - k) % 4
        for z in range(4):
            for q in range(CAP):
                want = asked[k][facts[PLACE + 3] * 4 + z, q : q + 1, :]
                block = jnp.zeros((NV, TILE), F32)
                for b in range(SEGB):
                    block = jnp.where(want == b, line[z, :, b * TILE : (b + 1) * TILE], block)
                message[to, z, q * NV : (q + 1) * NV, :] = block


def pack(facts, line, asked):
    return pl.pallas_call(
        pack_kernel,
        out_shape=jax.ShapeDtypeStruct((4, 4, CAP * NV, TILE), F32),
        in_specs=[sspec()] + [vspec()] * 5,
        out_specs=vspec(),
        compiler_params=params(8),
        cost_estimate=hint(1),
        name="pack",
    )(facts, line, *asked)


def split(x):
    high = x.astype(BF16)
    return high, (x - high.astype(F32)).astype(BF16)


def tile_loop(count, tiles, held, sems, slot):
    def copy(k):
        return pltpu.make_async_copy(tiles.at[k], held.at[k], sems.at[k])

    def start(k, _):
        copy(k).start()
        return 0

    def one(k):
        slot(k, *split(held[k]))

    def group(g, _):
        for u in range(UNROLL):
            copy(g * UNROLL + u).wait()
        for u in range(UNROLL):
            one(g * UNROLL + u)
        return 0

    def single(k, _):
        copy(k).wait()
        one(k)
        return 0

    def run():
        whole = count // UNROLL
        lax.fori_loop(0, whole, group, 0)
        lax.fori_loop(whole * UNROLL, count, single, 0)

    lax.fori_loop(0, count, start, 0)
    return run


def put(vecs, at, block):
    high, low = split(block)
    vecs[at, 0:NV, :] = high
    vecs[at, NV : 2 * NV, :] = low


def rows_kernel(first, *refs):
    facts, slots, ids, tiles = refs[:4]
    from_y = refs[4:12]
    to_x, held, sems, vecs, total = refs[12:]

    def slot(k, high, low):
        i = slots[0, k]
        v = vecs[slots[1, k]]
        a = lax.dot_general(v, high, ACROSS, preferred_element_type=F32)
        b = lax.dot_general(v[:NV], low, ACROSS, preferred_element_type=F32)
        total[i] += a[:NV] + a[NV:] + b

    run = tile_loop(facts[COUNT], tiles, held, sems, slot)
    n_segs = to_x.shape[0]
    for p in range(8):
        for h in range(2):
            for b in range(SEGB):
                at = (p * 2 + h) * SEGB + b
                if first:
                    put(vecs, at, from_y[p][h, :, b * TILE : (b + 1) * TILE])
                else:
                    put(vecs, at, from_y[p][(h * SEGB + b) * NV : (h * SEGB + b + 1) * NV, :])
    total[...] = jnp.zeros(total.shape, F32)
    run()
    if not first:
        carried = from_y[0][2 * SEG : 2 * SEG + RID, :]
        for p in range(1, 8):
            carried = carried + from_y[p][2 * SEG : 2 * SEG + RID, :]
    for s in range(n_segs):
        for q in range(CAP):
            to_x[s, q * NV : (q + 1) * NV, :] = total[s * CAP + q]
        if first:
            carried = ids[s]
        to_x[s, CAP * NV : CAP * NV + RID, :] = carried


def cols_kernel(*refs):
    facts, slots, tiles, from_x = refs[:4]
    to_y = refs[4:12]
    held, sems, vecs, total = refs[12:]

    def slot(k, high, low):
        j = slots[1, k]
        v = vecs[slots[0, k]]
        a = jnp.dot(v, high, preferred_element_type=F32)
        b = jnp.dot(v[:NV], low, preferred_element_type=F32)
        total[j] += a[:NV] + a[NV:] + b

    run = tile_loop(facts[COUNT], tiles, held, sems, slot)
    for s in range(from_x.shape[0]):
        for q in range(CAP):
            put(vecs, s * CAP + q, from_x[s, q * NV : (q + 1) * NV, :])
    total[...] = jnp.zeros(total.shape, F32)
    run()
    for p in range(8):
        for b in range(2 * SEGB):
            to_y[p][b * NV : (b + 1) * NV, :] = total[p * 2 * SEGB + b]


def tile_scratch(tiles):
    return [pltpu.VMEM(tiles.shape, F32), pltpu.SemaphoreType.DMA(tiles.shape[:1])]


def rows_product(facts, slots, ids, tiles, from_y, first):
    def kernel(*refs):
        rows_kernel(first, *refs)

    return pl.pallas_call(
        kernel,
        out_shape=jax.ShapeDtypeStruct((16, CAP * NV + RID, TILE), F32),
        in_specs=[sspec()] * 2 + [vspec(), pl.BlockSpec(memory_space=pltpu.HBM)] + [vspec()] * 8,
        out_specs=vspec(),
        scratch_shapes=tile_scratch(tiles)
        + [pltpu.VMEM((16 * SEGB, 2 * NV, TILE), BF16), pltpu.VMEM((16 * CAP, NV, TILE), F32)],
        compiler_params=params(24),
        cost_estimate=hint(4 if first else 5),
        name="rows_product",
    )(facts, slots, ids, tiles, *from_y)


def cols_product(facts, slots, tiles, from_x):
    return pl.pallas_call(
        cols_kernel,
        out_shape=(jax.ShapeDtypeStruct((2 * SEG, TILE), F32),) * 8,
        in_specs=[sspec()] * 2 + [pl.BlockSpec(memory_space=pltpu.HBM), vspec()],
        out_specs=(vspec(),) * 8,
        scratch_shapes=tile_scratch(tiles)
        + [
            pltpu.VMEM((16 * CAP, 2 * NV, TILE), BF16),
            pltpu.VMEM((16 * SEGB, NV, TILE), F32),
        ],
        compiler_params=params(24),
        cost_estimate=hint(5),
        name="cols_product",
    )(facts, slots, tiles, from_x)


def add_terms(wanted, from_x, total):
    for b in range(SEGB):
        at = slice(b * NV, (b + 1) * NV)
        block = total[at, :]
        for d in range(from_x.shape[0]):
            for q in range(CAP):
                term = from_x[d, q * NV : (q + 1) * NV, :]
                block = block + jnp.where(wanted[d, q : q + 1, :] == b, term, 0.0)
        total[at, :] = block


def near_kernel(from_x, wanted, total):
    total[...] = jnp.zeros(total.shape, F32)
    wanted[...] = from_x[:, CAP * NV : CAP * NV + RID, :]
    add_terms(wanted, from_x, total)


def near(from_x):
    return pl.pallas_call(
        near_kernel,
        out_shape=(
            jax.ShapeDtypeStruct((from_x.shape[0], RID, TILE), F32),
            jax.ShapeDtypeStruct((SEG, TILE), F32),
        ),
        in_specs=[vspec()],
        out_specs=(vspec(), vspec()),
        compiler_params=params(8),
        name="near",
    )(from_x)


def turn_kernel(wanted, near_mine, far_mine, far_theirs, product, message):
    for b in range(SEGB):
        at = slice(b * NV, (b + 1) * NV)
        product[at, :] = near_mine[at, :] + (far_mine[at, :] + far_theirs[at, :])
    for d in range(message.shape[0]):
        for q in range(CAP):
            want = wanted[d, q : q + 1, :]
            block = jnp.zeros((NV, TILE), F32)
            for b in range(SEGB):
                block = jnp.where(want == b, product[b * NV : (b + 1) * NV, :], block)
            message[d, q * NV : (q + 1) * NV, :] = block


def turn(wanted, near_mine, far_mine, far_theirs):
    return pl.pallas_call(
        turn_kernel,
        out_shape=(
            jax.ShapeDtypeStruct((SEG, TILE), F32),
            jax.ShapeDtypeStruct((wanted.shape[0], CAP * NV, TILE), F32),
        ),
        in_specs=[vspec()] * 4,
        out_specs=(vspec(), vspec()),
        compiler_params=params(8),
        name="turn",
    )(wanted, near_mine, far_mine, far_theirs)


def cross(a, b):
    return lax.dot_general(a, b, ACROSS, precision=HIGH, preferred_element_type=F32)


def fan_kernel(mine, theirs, pair, correlation):
    pair[0] = mine[...]
    pair[1] = theirs[...]
    correlation[...] = cross(mine[...], mine[...]) + cross(theirs[...], theirs[...])


def fan(mine, theirs):
    return pl.pallas_call(
        fan_kernel,
        out_shape=(
            jax.ShapeDtypeStruct((2,) + mine.shape, F32),
            jax.ShapeDtypeStruct((NV, NV), F32),
        ),
        in_specs=[vspec()] * 2,
        out_specs=(vspec(),) * 2,
        compiler_params=params(8),
        cost_estimate=hint(5),
        name="fan",
    )(mine, theirs)


def load_kernel(product, other, mine, theirs, correlation, ride):
    ride[0:SEG, :] = product[...]
    ride[SEG : 2 * SEG, :] = other[...]
    projection = jnp.zeros((NV, NV), F32)
    for h, vectors in enumerate((mine, theirs)):
        for b in range(SEGB):
            at = (h * SEGB + b) * NV
            projection += cross(vectors[:, b * TILE : (b + 1) * TILE], ride[at : at + NV, :])
    ride[2 * SEG : 2 * SEG + RID, :] = jnp.zeros((RID, TILE), F32)
    for at, matrix in ((0, correlation[...]), (2, projection)):
        for h in range(2):
            ride[2 * SEG : 2 * SEG + RID, (at + h) * NV : (at + h + 1) * NV] = matrix[h * RID : (h + 1) * RID, :]


def load(product, other, mine, theirs, correlation):
    return pl.pallas_call(
        load_kernel,
        out_shape=jax.ShapeDtypeStruct((2 * SEG + RID, TILE), F32),
        in_specs=[vspec()] * 5,
        out_specs=vspec(),
        compiler_params=params(4),
        cost_estimate=hint(50),
        name="load",
    )(product, other, mine, theirs, correlation)


def solve(correlation, projection):
    m = jnp.concatenate([correlation, projection], axis=1)
    row_id = lax.broadcasted_iota(jnp.int32, m.shape, 0)
    for j in range(NV):
        row = m[j : j + 1, :] / m[j : j + 1, j : j + 1]
        m = jnp.where(row_id == j, row, m - m[:, j : j + 1] * row)
    return m[:, NV:]


def thirds(x):
    high = x.astype(BF16)
    rest = x - high.astype(F32)
    middle = rest.astype(BF16)
    return high, middle, (rest - middle.astype(F32)).astype(BF16)


def stack_left(x):
    a, b, c = thirds(x)
    return jnp.concatenate([a, a, b, a, b, c], axis=1)


def times(left, x):
    a, b, c = thirds(x)
    right = jnp.concatenate([a, b, a, c, b, a], axis=0)
    return jnp.dot(left, right, preferred_element_type=F32)


def finish_kernel(wanted, from_x, both, mine, theirs, pair, residual, image, gram, total):
    total[...] = both[0:SEG, :]
    add_terms(wanted, from_x, total)
    carried = from_x[0, CAP * NV : CAP * NV + RID, :]
    for d in range(1, from_x.shape[0]):
        carried = carried + from_x[d, CAP * NV : CAP * NV + RID, :]
    correlation, projection = (
        jnp.concatenate([carried[:, (at + h) * NV : (at + h + 1) * NV] for h in range(2)], axis=0) for at in (0, 2)
    )
    coeffs = solve(correlation, projection)
    back = stack_left(coeffs.T)
    local = jnp.zeros((NV, NV), F32)
    for b in range(SEGB):
        at = slice(b * NV, (b + 1) * NV)
        other = slice(SEG + b * NV, SEG + (b + 1) * NV)
        cols = slice(b * TILE, (b + 1) * TILE)
        p = pair[at, :]
        r = p - times(back, mine[:, cols])
        m = total[at, :] - times(back, p)
        residual[:, cols] = r
        image[:, cols] = m
        r_other = pair[other, :] - times(back, theirs[:, cols])
        local += cross(r, m) + cross(r_other, both[other, :])
    for h in range(2):
        for r in range(RID):
            gram[h : h + 1, r * NV : (r + 1) * NV] = local[h * RID + r : h * RID + r + 1, :]


def finish(wanted, from_x, both, mine, theirs, pair):
    return pl.pallas_call(
        finish_kernel,
        out_shape=(
            jax.ShapeDtypeStruct(mine.shape, F32),
            jax.ShapeDtypeStruct(mine.shape, F32),
            jax.ShapeDtypeStruct((2, 128), F32),
        ),
        in_specs=[vspec()] * 6,
        out_specs=(vspec(),) * 3,
        scratch_shapes=[pltpu.VMEM((SEG, TILE), F32)],
        compiler_params=params(8),
        name="finish",
    )(wanted, from_x, both, mine, theirs, pair)


def last_kernel(part, far, image):
    for b in range(SEGB):
        cols = slice(b * TILE, (b + 1) * TILE)
        image[:, cols] = part[:, cols] + far[b * NV : (b + 1) * NV, :]


def last(part, far):
    return pl.pallas_call(
        last_kernel,
        out_shape=jax.ShapeDtypeStruct(part.shape, F32),
        in_specs=[vspec()] * 2,
        out_specs=vspec(),
        compiler_params=params(4),
        cost_estimate=hint(5),
        name="last",
    )(part, far)


def in_hbm(x):
    return pltpu.with_memory_space_constraint(x, pltpu.HBM)


def swap(x, axis):
    return lax.all_to_all(x, axis, 0, 0, tiled=True)


def other_half(x):
    return lax.ppermute(x, "zh", turned(2, 1))


def other_core(x):
    return lax.ppermute(x, "core", turned(2, 1))


def spread(mine):
    pieces = [mine] + [lax.ppermute(mine, "y", turned(4, -step)) for step in (1, 2, 3)]
    return pieces + [other_core(x) for x in pieces]


def collect(pieces):
    met = [a + other_core(b) for a, b in zip(pieces[:4], pieces[4:])]
    both = met[0]
    for step in (1, 2, 3):
        both = both + lax.ppermute(met[step], "y", turned(4, step))
    return both


def per_device(vectors, tiles, tile_rows, tile_cols, counts):
    cell_tiles = in_hbm(tiles[0, 0])
    order_total = vectors.shape[1] * lax.axis_size(ROW) * lax.axis_size(COL)
    place = jnp.stack([lax.axis_index(name).astype(jnp.int32) for name in ROW + ("x",)])
    facts = jnp.concatenate([tile_rows.reshape(MAXT), tile_cols.reshape(MAXT), counts.reshape(1), place])
    slots, ids = prep(facts)
    asked = [ids] + [lax.ppermute(ids, "x", turned(4, k)) for k in (1, 2, 3)]

    theirs = other_half(vectors)
    both, correlation = fan(in_hbm(vectors), theirs)
    from_y = spread(both)
    line = swap(jnp.broadcast_to(vectors, (4,) + vectors.shape), "zl")
    from_x = swap(pack(facts, line, asked), "x").reshape(16, CAP * NV, TILE)
    to_x = rows_product(facts, slots, ids, cell_tiles, from_y, True)
    to_y = cols_product(facts, slots, cell_tiles, from_x)
    from_x = swap(to_x, COL)
    both = collect(to_y)
    far = other_half(both[SEG:])
    wanted, mine = near(from_x)
    product, message = turn(wanted, mine, both, far)

    from_x = swap(message, COL)
    pair = load(product, other_half(product), vectors, theirs, correlation)
    from_y = spread(pair)
    to_x = rows_product(facts, slots, ids, cell_tiles, from_y, False)
    to_y = cols_product(facts, slots, cell_tiles, from_x)
    from_x = swap(to_x, COL)
    both = collect(to_y)
    residual, part, local = finish(wanted, from_x, both, vectors, theirs, pair)
    image = last(part, other_half(both[SEG:]))

    chip = local + other_core(local)
    copies = jnp.broadcast_to(chip, (128,) + chip.shape)
    gram = jnp.sum(swap(copies, ("y", "zh", "x", "zl")), axis=0).reshape(NV, NV) / order_total
    return (residual, image, gram)


def solution(mesh):
    fine = Mesh(mesh.devices.reshape(ROW_SIZES + COL_SIZES), ROW + COL)
    in_specs = (
        P(None, ROW + COL),
        P(ROW, COL, None, None, None),
        P(ROW, COL, None),
        P(ROW, COL, None),
        P(ROW, COL),
    )
    out_specs = (P(None, ROW + COL), P(None, ROW + COL), P())
    return jax.shard_map(
        per_device, mesh=fine, in_specs=in_specs, out_specs=out_specs, check_vma=False
    )
```

```python
import jax
import jax.numpy as jnp
from jax import lax
from jax.experimental import pallas as pl
from jax.experimental.pallas import tpu as pltpu
from jax.sharding import Mesh
from jax.sharding import PartitionSpec as P


ROW = ("y", "zh", "core")
COL = ("x", "zl")
ROW_SIZES = (4, 2, 2)
COL_SIZES = (4, 4)
NV = 16
TILE = 256
SEGB = 6
CAP = 3
SEG = SEGB * NV
RID = 8
MAXT = 48
COUNT = 2 * MAXT
PLACE = COUNT + 1
UNROLL = 4
F32 = jnp.float32
BF16 = jnp.bfloat16
HIGH = lax.Precision.HIGHEST
ACROSS = (((1,), (1,)), ((), ()))
MIB = 1024 * 1024


def vspec():
    return pl.BlockSpec(memory_space=pltpu.VMEM)


def sspec():
    return pl.BlockSpec(memory_space=pltpu.SMEM)


def hint(us):
    return pl.CostEstimate(flops=int(us * 1e9), bytes_accessed=0, transcendentals=0)


def params(mib):
    return pltpu.CompilerParams(vmem_limit_bytes=mib * MIB)


def turned(n, step):
    return [(i, (i + step) % n) for i in range(n)]


def prep_kernel(facts, slots, ids, table, mark, used):
    n_segs = used.shape[0]

    def clear(b, _):
        mark[b] = -1
        return 0

    lax.fori_loop(0, n_segs * SEGB, clear, 0)

    def clear_table(s, _):
        used[s] = 0
        for q in range(CAP):
            table[s * CAP + q] = 0
        return 0

    lax.fori_loop(0, n_segs, clear_table, 0)
    count, my_y, my_half, my_core = facts[COUNT], facts[PLACE], facts[PLACE + 1], facts[PLACE + 2]

    def slot(k, _):
        b = facts[k]
        s = b // SEGB
        old = mark[b]
        rank = jnp.where(old < 0, used[s], old)
        mark[b] = rank
        used[s] = jnp.where(old < 0, rank + 1, used[s])
        table[s * CAP + rank] = b - s * SEGB
        slots[0, k] = s * CAP + rank
        g = facts[MAXT + k]
        t = g // SEGB
        step = (t // 4 + 4 - my_y) % 4
        half = (t // 2 % 2 + my_half) % 2
        core = (t % 2 + my_core) % 2
        slots[1, k] = ((core * 4 + step) * 2 + half) * SEGB + g - t * SEGB
        return 0

    lax.fori_loop(0, count, slot, 0)
    row_id = lax.broadcasted_iota(jnp.int32, (RID, TILE), 0)

    for s in range(n_segs):
        out = jnp.zeros((RID, TILE), jnp.int32)
        for q in range(CAP):
            out = jnp.where(row_id == q, table[s * CAP + q], out)
        ids[s] = out.astype(F32)


def prep(facts):
    n_segs = 16
    return pl.pallas_call(
        prep_kernel,
        out_shape=(
            jax.ShapeDtypeStruct((2, MAXT), jnp.int32),
            jax.ShapeDtypeStruct((n_segs, RID, TILE), F32),
        ),
        in_specs=[sspec()],
        out_specs=(sspec(), vspec()),
        scratch_shapes=[
            pltpu.SMEM((n_segs * CAP,), jnp.int32),
            pltpu.SMEM((n_segs * SEGB,), jnp.int32),
            pltpu.SMEM((n_segs,), jnp.int32),
        ],
        compiler_params=params(4),
        cost_estimate=hint(2),
        name="prep",
    )(facts)


def pack_kernel(facts, line, *refs):
    asked, message = refs[:4], refs[4]
    for k in range(4):
        to = (facts[PLACE + 3] + 4 - k) % 4
        for z in range(4):
            for q in range(CAP):
                want = asked[k][facts[PLACE + 3] * 4 + z, q : q + 1, :]
                block = jnp.zeros((NV, TILE), F32)
                for b in range(SEGB):
                    block = jnp.where(want == b, line[z, :, b * TILE : (b + 1) * TILE], block)
                message[to, z, q * NV : (q + 1) * NV, :] = block


def pack(facts, line, asked):
    return pl.pallas_call(
        pack_kernel,
        out_shape=jax.ShapeDtypeStruct((4, 4, CAP * NV, TILE), F32),
        in_specs=[sspec()] + [vspec()] * 5,
        out_specs=vspec(),
        compiler_params=params(8),
        cost_estimate=hint(1),
        name="pack",
    )(facts, line, *asked)


def split(x):
    high = x.astype(BF16)
    return high, (x - high.astype(F32)).astype(BF16)


def tile_loop(count, tiles, held, sems, slot):
    def copy(k):
        return pltpu.make_async_copy(tiles.at[k], held.at[k], sems.at[k])

    def start(k, _):
        copy(k).start()
        return 0

    def one(k):
        slot(k, *split(held[k]))

    def group(g, _):
        for u in range(UNROLL):
            copy(g * UNROLL + u).wait()
        for u in range(UNROLL):
            one(g * UNROLL + u)
        return 0

    def single(k, _):
        copy(k).wait()
        one(k)
        return 0

    def run():
        whole = count // UNROLL
        lax.fori_loop(0, whole, group, 0)
        lax.fori_loop(whole * UNROLL, count, single, 0)

    lax.fori_loop(0, count, start, 0)
    return run


def put(vecs, at, block):
    high, low = split(block)
    vecs[at, 0:NV, :] = high
    vecs[at, NV : 2 * NV, :] = low


def rows_kernel(first, *refs):
    facts, slots, ids, tiles = refs[:4]
    from_y = refs[4:12]
    to_x, held, sems, vecs, total = refs[12:]

    def slot(k, high, low):
        i = slots[0, k]
        v = vecs[slots[1, k]]
        a = lax.dot_general(v, high, ACROSS, preferred_element_type=F32)
        b = lax.dot_general(v[:NV], low, ACROSS, preferred_element_type=F32)
        total[i] += a[:NV] + a[NV:] + b

    run = tile_loop(facts[COUNT], tiles, held, sems, slot)
    n_segs = to_x.shape[0]
    for p in range(8):
        for h in range(2):
            for b in range(SEGB):
                at = (p * 2 + h) * SEGB + b
                if first:
                    put(vecs, at, from_y[p][h, :, b * TILE : (b + 1) * TILE])
                else:
                    put(vecs, at, from_y[p][(h * SEGB + b) * NV : (h * SEGB + b + 1) * NV, :])
    total[...] = jnp.zeros(total.shape, F32)
    run()
    if not first:
        carried = from_y[0][2 * SEG : 2 * SEG + RID, :]
        for p in range(1, 8):
            carried = carried + from_y[p][2 * SEG : 2 * SEG + RID, :]
    for s in range(n_segs):
        for q in range(CAP):
            to_x[s, q * NV : (q + 1) * NV, :] = total[s * CAP + q]
        if first:
            carried = ids[s]
        to_x[s, CAP * NV : CAP * NV + RID, :] = carried


def cols_kernel(*refs):
    facts, slots, tiles, from_x = refs[:4]
    to_y = refs[4:12]
    held, sems, vecs, total = refs[12:]

    def slot(k, high, low):
        j = slots[1, k]
        v = vecs[slots[0, k]]
        a = jnp.dot(v, high, preferred_element_type=F32)
        b = jnp.dot(v[:NV], low, preferred_element_type=F32)
        total[j] += a[:NV] + a[NV:] + b

    run = tile_loop(facts[COUNT], tiles, held, sems, slot)
    for s in range(from_x.shape[0]):
        for q in range(CAP):
            put(vecs, s * CAP + q, from_x[s, q * NV : (q + 1) * NV, :])
    total[...] = jnp.zeros(total.shape, F32)
    run()
    for p in range(8):
        for b in range(2 * SEGB):
            to_y[p][b * NV : (b + 1) * NV, :] = total[p * 2 * SEGB + b]


def tile_scratch(tiles):
    return [pltpu.VMEM(tiles.shape, F32), pltpu.SemaphoreType.DMA(tiles.shape[:1])]


def rows_product(facts, slots, ids, tiles, from_y, first):
    def kernel(*refs):
        rows_kernel(first, *refs)

    return pl.pallas_call(
        kernel,
        out_shape=jax.ShapeDtypeStruct((16, CAP * NV + RID, TILE), F32),
        in_specs=[sspec()] * 2 + [vspec(), pl.BlockSpec(memory_space=pltpu.HBM)] + [vspec()] * 8,
        out_specs=vspec(),
        scratch_shapes=tile_scratch(tiles)
        + [pltpu.VMEM((16 * SEGB, 2 * NV, TILE), BF16), pltpu.VMEM((16 * CAP, NV, TILE), F32)],
        compiler_params=params(24),
        cost_estimate=hint(4 if first else 5),
        name="rows_product",
    )(facts, slots, ids, tiles, *from_y)


def cols_product(facts, slots, tiles, from_x):
    return pl.pallas_call(
        cols_kernel,
        out_shape=(jax.ShapeDtypeStruct((2 * SEG, TILE), F32),) * 8,
        in_specs=[sspec()] * 2 + [pl.BlockSpec(memory_space=pltpu.HBM), vspec()],
        out_specs=(vspec(),) * 8,
        scratch_shapes=tile_scratch(tiles)
        + [
            pltpu.VMEM((16 * CAP, 2 * NV, TILE), BF16),
            pltpu.VMEM((16 * SEGB, NV, TILE), F32),
        ],
        compiler_params=params(24),
        cost_estimate=hint(5),
        name="cols_product",
    )(facts, slots, tiles, from_x)


def add_terms(wanted, from_x, total):
    for b in range(SEGB):
        at = slice(b * NV, (b + 1) * NV)
        block = total[at, :]
        for d in range(from_x.shape[0]):
            for q in range(CAP):
                term = from_x[d, q * NV : (q + 1) * NV, :]
                block = block + jnp.where(wanted[d, q : q + 1, :] == b, term, 0.0)
        total[at, :] = block


def near_kernel(from_x, wanted, total):
    total[...] = jnp.zeros(total.shape, F32)
    wanted[...] = from_x[:, CAP * NV : CAP * NV + RID, :]
    add_terms(wanted, from_x, total)


def near(from_x):
    return pl.pallas_call(
        near_kernel,
        out_shape=(
            jax.ShapeDtypeStruct((from_x.shape[0], RID, TILE), F32),
            jax.ShapeDtypeStruct((SEG, TILE), F32),
        ),
        in_specs=[vspec()],
        out_specs=(vspec(), vspec()),
        compiler_params=params(8),
        name="near",
    )(from_x)


def turn_kernel(wanted, near_mine, far_mine, far_theirs, product, message):
    for b in range(SEGB):
        at = slice(b * NV, (b + 1) * NV)
        product[at, :] = near_mine[at, :] + (far_mine[at, :] + far_theirs[at, :])
    for d in range(message.shape[0]):
        for q in range(CAP):
            want = wanted[d, q : q + 1, :]
            block = jnp.zeros((NV, TILE), F32)
            for b in range(SEGB):
                block = jnp.where(want == b, product[b * NV : (b + 1) * NV, :], block)
            message[d, q * NV : (q + 1) * NV, :] = block


def turn(wanted, near_mine, far_mine, far_theirs):
    return pl.pallas_call(
        turn_kernel,
        out_shape=(
            jax.ShapeDtypeStruct((SEG, TILE), F32),
            jax.ShapeDtypeStruct((wanted.shape[0], CAP * NV, TILE), F32),
        ),
        in_specs=[vspec()] * 4,
        out_specs=(vspec(), vspec()),
        compiler_params=params(8),
        name="turn",
    )(wanted, near_mine, far_mine, far_theirs)


def cross(a, b):
    return lax.dot_general(a, b, ACROSS, precision=HIGH, preferred_element_type=F32)


def fan_kernel(mine, theirs, pair, correlation):
    pair[0] = mine[...]
    pair[1] = theirs[...]
    correlation[...] = cross(mine[...], mine[...]) + cross(theirs[...], theirs[...])


def fan(mine, theirs):
    return pl.pallas_call(
        fan_kernel,
        out_shape=(
            jax.ShapeDtypeStruct((2,) + mine.shape, F32),
            jax.ShapeDtypeStruct((NV, NV), F32),
        ),
        in_specs=[vspec()] * 2,
        out_specs=(vspec(),) * 2,
        compiler_params=params(8),
        cost_estimate=hint(5),
        name="fan",
    )(mine, theirs)


def load_kernel(product, other, mine, theirs, correlation, ride):
    ride[0:SEG, :] = product[...]
    ride[SEG : 2 * SEG, :] = other[...]
    projection = jnp.zeros((NV, NV), F32)
    for h, vectors in enumerate((mine, theirs)):
        for b in range(SEGB):
            at = (h * SEGB + b) * NV
            projection += cross(vectors[:, b * TILE : (b + 1) * TILE], ride[at : at + NV, :])
    ride[2 * SEG : 2 * SEG + RID, :] = jnp.zeros((RID, TILE), F32)
    for at, matrix in ((0, correlation[...]), (2, projection)):
        for h in range(2):
            ride[2 * SEG : 2 * SEG + RID, (at + h) * NV : (at + h + 1) * NV] = matrix[h * RID : (h + 1) * RID, :]


def load(product, other, mine, theirs, correlation):
    return pl.pallas_call(
        load_kernel,
        out_shape=jax.ShapeDtypeStruct((2 * SEG + RID, TILE), F32),
        in_specs=[vspec()] * 5,
        out_specs=vspec(),
        compiler_params=params(4),
        cost_estimate=hint(50),
        name="load",
    )(product, other, mine, theirs, correlation)


def solve(correlation, projection):
    m = jnp.concatenate([correlation, projection], axis=1)
    row_id = lax.broadcasted_iota(jnp.int32, m.shape, 0)
    for j in range(NV):
        row = m[j : j + 1, :] / m[j : j + 1, j : j + 1]
        m = jnp.where(row_id == j, row, m - m[:, j : j + 1] * row)
    return m[:, NV:]


def thirds(x):
    high = x.astype(BF16)
    rest = x - high.astype(F32)
    middle = rest.astype(BF16)
    return high, middle, (rest - middle.astype(F32)).astype(BF16)


def stack_left(x):
    a, b, c = thirds(x)
    return jnp.concatenate([a, a, b, a, b, c], axis=1)


def times(left, x):
    a, b, c = thirds(x)
    right = jnp.concatenate([a, b, a, c, b, a], axis=0)
    return jnp.dot(left, right, preferred_element_type=F32)


def finish_kernel(wanted, from_x, both, mine, theirs, pair, residual, image, gram, total):
    total[...] = both[0:SEG, :]
    add_terms(wanted, from_x, total)
    carried = from_x[0, CAP * NV : CAP * NV + RID, :]
    for d in range(1, from_x.shape[0]):
        carried = carried + from_x[d, CAP * NV : CAP * NV + RID, :]
    correlation, projection = (
        jnp.concatenate([carried[:, (at + h) * NV : (at + h + 1) * NV] for h in range(2)], axis=0) for at in (0, 2)
    )
    coeffs = solve(correlation, projection)
    back = stack_left(coeffs.T)
    local = jnp.zeros((NV, NV), F32)
    for b in range(SEGB):
        at = slice(b * NV, (b + 1) * NV)
        other = slice(SEG + b * NV, SEG + (b + 1) * NV)
        cols = slice(b * TILE, (b + 1) * TILE)
        p = pair[at, :]
        r = p - times(back, mine[:, cols])
        m = total[at, :] - times(back, p)
        residual[:, cols] = r
        image[:, cols] = m
        r_other = pair[other, :] - times(back, theirs[:, cols])
        local += cross(r, m) + cross(r_other, both[other, :])
    for h in range(2):
        for r in range(RID):
            gram[h : h + 1, r * NV : (r + 1) * NV] = local[h * RID + r : h * RID + r + 1, :]


def finish(wanted, from_x, both, mine, theirs, pair):
    return pl.pallas_call(
        finish_kernel,
        out_shape=(
            jax.ShapeDtypeStruct(mine.shape, F32),
            jax.ShapeDtypeStruct(mine.shape, F32),
            jax.ShapeDtypeStruct((2, 128), F32),
        ),
        in_specs=[vspec()] * 6,
        out_specs=(vspec(),) * 3,
        scratch_shapes=[pltpu.VMEM((SEG, TILE), F32)],
        compiler_params=params(8),
        name="finish",
    )(wanted, from_x, both, mine, theirs, pair)


def last_kernel(part, far, image):
    for b in range(SEGB):
        cols = slice(b * TILE, (b + 1) * TILE)
        image[:, cols] = part[:, cols] + far[b * NV : (b + 1) * NV, :]


def last(part, far):
    return pl.pallas_call(
        last_kernel,
        out_shape=jax.ShapeDtypeStruct(part.shape, F32),
        in_specs=[vspec()] * 2,
        out_specs=vspec(),
        compiler_params=params(4),
        name="last",
    )(part, far)


def in_hbm(x):
    return pltpu.with_memory_space_constraint(x, pltpu.HBM)


def swap(x, axis):
    return lax.all_to_all(x, axis, 0, 0, tiled=True)


def other_half(x):
    return lax.ppermute(x, "zh", turned(2, 1))


def other_core(x):
    return lax.ppermute(x, "core", turned(2, 1))


def spread(mine):
    pieces = [mine] + [lax.ppermute(mine, "y", turned(4, -step)) for step in (1, 2, 3)]
    return pieces + [other_core(x) for x in pieces]


def collect(pieces):
    met = [a + other_core(b) for a, b in zip(pieces[:4], pieces[4:])]
    both = met[0]
    for step in (1, 2, 3):
        both = both + lax.ppermute(met[step], "y", turned(4, step))
    return both


def per_device(vectors, tiles, tile_rows, tile_cols, counts):
    cell_tiles = in_hbm(tiles[0, 0])
    order_total = vectors.shape[1] * lax.axis_size(ROW) * lax.axis_size(COL)
    place = jnp.stack([lax.axis_index(name).astype(jnp.int32) for name in ROW + ("x",)])
    facts = jnp.concatenate([tile_rows.reshape(MAXT), tile_cols.reshape(MAXT), counts.reshape(1), place])
    slots, ids = prep(facts)
    asked = [ids] + [lax.ppermute(ids, "x", turned(4, k)) for k in (1, 2, 3)]

    theirs = other_half(vectors)
    both, correlation = fan(in_hbm(vectors), theirs)
    from_y = spread(both)
    line = swap(jnp.broadcast_to(vectors, (4,) + vectors.shape), "zl")
    from_x = swap(pack(facts, line, asked), "x").reshape(16, CAP * NV, TILE)
    to_x = rows_product(facts, slots, ids, cell_tiles, from_y, True)
    to_y = cols_product(facts, slots, cell_tiles, from_x)
    from_x = swap(to_x, COL)
    both = collect(to_y)
    far = other_half(both[SEG:])
    wanted, mine = near(from_x)
    product, message = turn(wanted, mine, both, far)

    from_x = swap(message, COL)
    pair = load(product, other_half(product), vectors, theirs, correlation)
    from_y = spread(pair)
    to_x = rows_product(facts, slots, ids, cell_tiles, from_y, False)
    to_y = cols_product(facts, slots, cell_tiles, from_x)
    from_x = swap(to_x, COL)
    both = collect(to_y)
    residual, part, local = finish(wanted, from_x, both, vectors, theirs, pair)
    image = last(part, other_half(both[SEG:]))

    chip = local + other_core(local)
    copies = jnp.broadcast_to(chip, (128,) + chip.shape)
    gram = jnp.sum(swap(copies, ("y", "zh", "x", "zl")), axis=0).reshape(NV, NV) / order_total
    return (residual, image, gram)


def solution(mesh):
    fine = Mesh(mesh.devices.reshape(ROW_SIZES + COL_SIZES), ROW + COL)
    in_specs = (
        P(None, ROW + COL),
        P(ROW, COL, None, None, None),
        P(ROW, COL, None),
        P(ROW, COL, None),
        P(ROW, COL),
    )
    out_specs = (P(None, ROW + COL), P(None, ROW + COL), P())
    return jax.shard_map(
        per_device, mesh=fine, in_specs=in_specs, out_specs=out_specs, check_vma=False
    )
```
